256 devices in a mesh: row: 16 (over x_hi, z), col: 16 (over y, x_lo, core).
Axes of the slice: x: 4 (x_hi: 2, x_lo: 2; x = x_hi * 2 + x_lo), y: 4, z: 8, core: 2. Of those that a mesh axis runs over, the one named last changes fastest.
Arguments:
- pair: bfloat16 [512, 512, 128], P('row', 'col'), may hold values from -6 to 6
- residue_mask: int32 [512], replicated, may hold values 0 or 1
- cotangent: bfloat16 [512, 512, 128], P('row', 'col'), may hold values from -6 to 6
- w_in: bfloat16 [128, 512], replicated, may hold values from -0.5 to 0.5
- w_out: bfloat16 [128, 128], replicated, may hold values from -0.5 to 0.5
- w_gout: bfloat16 [128, 128], replicated, may hold values from -0.5 to 0.5
- gain_in: float32 [128], replicated, may hold values from 0.25 to 1.75
- bias_in: float32 [128], replicated, may hold values from -3 to 3
- gain_out: float32 [128], replicated, may hold values from 0.25 to 1.75
- bias_out: float32 [128], replicated, may hold values from -3 to 3
Outputs:
- output: bfloat16 [512, 512, 128], P('row', 'col')
- grad_pair: bfloat16 [512, 512, 128], P('row', 'col')
The draws below stay inside these ranges and needn't reach their ends.
All inputs are finite; a program needn't handle non-finite values.
Results may differ from the reference program's by a relative error of at most 0.017.
Values may be sent and summed in bfloat16 or wider, within the bound.
A program may use at most 128 MiB of HBM per device.

```python
import jax
import jax.numpy as jnp
from jax import lax

C = 128
H = 128
N = 512


def set_ends(array, own_key, smallest, high):
    longest = array.shape.index(max(array.shape))
    spots = []
    for shift in (0, 1):
        where = [jax.random.randint(jax.random.fold_in(own_key, axis), (), 0, length) for axis, length in enumerate(array.shape)]
        where[longest] = (where[longest] + shift) % array.shape[longest]
        spots.append(tuple(where))
    return array.at[spots[0]].set(smallest).at[spots[1]].set(high)


def shard_levels(key, shape, shards, least, largest):
    level = 1.0
    for axis_at, parts in shards:
        draws = jax.random.uniform(jax.random.fold_in(jax.random.fold_in(key, 6), axis_at), (parts,), jnp.float32, least / len(shards), largest / len(shards))
        level = level * jnp.repeat(jnp.exp(draws), shape[axis_at] // parts).reshape((-1,) + (1,) * (len(shape) - 1 - axis_at))
    return level


def bell_draw(rng, dims, deviation, most, pieces=(), dtype=jnp.bfloat16):
    drawn = jax.random.normal(rng, dims, jnp.float32) * deviation
    if len(pieces) > 0:
        drawn = shard_levels(rng, dims, pieces, -0.22, 0.18) * drawn
    return jnp.clip(drawn, min=-most, max=most).astype(dtype)


def setup_inputs(seed: int = 0) -> dict:
    seeds = jax.random.split(jax.random.key(seed), 11)
    pair = bell_draw(seeds[0], (N, N, C), 1.0, 6.0, ((0, 16), (1, 16)))
    residue_mask = set_ends((jax.random.randint(seeds[1], (N,), 0, 8) < 7).astype(jnp.int32), jax.random.fold_in(seeds[1], 1), 0, 1)
    cotangent = bell_draw(seeds[2], (N, N, C), 1.0, 6.0, ((0, 16), (1, 16)))
    w_in = bell_draw(seeds[3], (C, 4 * H), C ** -0.5, 0.5)
    w_out = bell_draw(seeds[4], (H, C), H ** -0.5, 0.5)
    w_gout = bell_draw(seeds[5], (C, C), C ** -0.5, 0.5)
    gain_in = jnp.clip(1.0 + 0.15 * jax.random.normal(seeds[6], (C,), jnp.float32), 0.25, 1.75)
    bias_in = bell_draw(seeds[7], (C,), 0.5, 3.0, (), jnp.float32)
    gain_out = jnp.clip(1.0 + 0.15 * jax.random.normal(seeds[8], (H,), jnp.float32), 0.25, 1.75)
    bias_out = bell_draw(seeds[9], (H,), 0.5, 3.0, (), jnp.float32)
    return dict(pair=pair, residue_mask=residue_mask, cotangent=cotangent, w_in=w_in, w_out=w_out, w_gout=w_gout, gain_in=gain_in, bias_in=bias_in, gain_out=gain_out, bias_out=bias_out)


epsilon = 1e-05

def normalize(values, gain_vec, offset):
    average = lax.optimization_barrier(jnp.mean(values, axis=-1, keepdims=True))
    centred = values - average
    inverse = lax.rsqrt(lax.optimization_barrier(jnp.mean(centred * centred, axis=-1, keepdims=True)) + epsilon)
    scaled = centred * inverse
    return (scaled * gain_vec + offset, scaled, inverse)

def norm_back(grad_norm, gain_vec, scaled, inverse):
    grad_scaled = grad_norm * gain_vec
    first_mean = lax.optimization_barrier(jnp.mean(grad_scaled, axis=-1, keepdims=True))
    second_mean = lax.optimization_barrier(jnp.mean(grad_scaled * scaled, axis=-1, keepdims=True))
    return (grad_scaled - first_mean - scaled * second_mean) * inverse

def reference(pair, residue_mask, cotangent, w_in, w_out, w_gout, gain_in, bias_in, gain_out, bias_out):
    hidden = w_out.shape[0]
    valid = residue_mask.astype(jnp.float32)
    pair_mask = (valid[:, None] * valid[None, :])[..., None]
    normed, scaled_in, inverse_in = normalize(pair.astype(jnp.float32), gain_in, bias_in)
    normed = normed.astype(jnp.bfloat16)
    mixed = jnp.dot(normed, w_in, preferred_element_type=jnp.float32)
    projected = mixed[..., :2 * hidden]
    gates = jax.nn.sigmoid(mixed[..., 2 * hidden:])
    branch = (gates * projected * pair_mask).astype(jnp.bfloat16)
    branch = lax.optimization_barrier(branch)
    left = branch[..., :hidden].astype(jnp.float32)
    right = branch[..., hidden:].astype(jnp.float32)
    tri = jnp.einsum('ikc,jkc->ijc', left, right, precision=lax.Precision.HIGHEST)
    out_norm, scaled_out, inverse_out = normalize(tri, gain_out, bias_out)
    out_norm = out_norm.astype(jnp.bfloat16)
    outer_gate = jax.nn.sigmoid(jnp.dot(normed, w_gout, preferred_element_type=jnp.float32))
    outer_proj = jnp.dot(out_norm, w_out, preferred_element_type=jnp.float32)
    output = (outer_gate * outer_proj).astype(jnp.bfloat16)
    upstream = cotangent.astype(jnp.float32)
    grad_proj = (upstream * outer_gate).astype(jnp.bfloat16)
    grad_gate = (upstream * outer_proj * outer_gate * (1.0 - outer_gate)).astype(jnp.bfloat16)
    grad_outnorm = jnp.dot(grad_proj, w_out.T, preferred_element_type=jnp.float32)
    grad_tri = norm_back(grad_outnorm, gain_out, scaled_out, inverse_out).astype(jnp.bfloat16)
    grad_tri = lax.optimization_barrier(grad_tri).astype(jnp.float32)
    grad_left = jnp.einsum('ijc,jkc->ikc', grad_tri, right, precision=lax.Precision.HIGHEST)
    grad_right = jnp.einsum('ijc,ikc->jkc', grad_tri, left, precision=lax.Precision.HIGHEST)
    grad_branch = jnp.concatenate([grad_left, grad_right], axis=-1) * pair_mask
    grad_mixed = jnp.concatenate([grad_branch * gates, grad_branch * projected * gates * (1.0 - gates)], axis=-1).astype(jnp.bfloat16)
    grad_normed = jnp.dot(grad_mixed, w_in.T, preferred_element_type=jnp.float32) + jnp.dot(grad_gate, w_gout.T, preferred_element_type=jnp.float32)
    grad_pair = norm_back(grad_normed, gain_in, scaled_in, inverse_in).astype(jnp.bfloat16)
    return (output, grad_pair)
```

```python
import jax
import jax.numpy as jnp
from jax import lax
from jax.sharding import PartitionSpec as P

epsilon = 1e-05


def normalize(values, gain_vec, offset):
    average = jnp.mean(values, axis=-1, keepdims=True)
    centred = values - average
    inverse = lax.rsqrt(jnp.mean(centred * centred, axis=-1, keepdims=True) + epsilon)
    scaled = centred * inverse
    return (scaled * gain_vec + offset, scaled, inverse)


def norm_back(grad_norm, gain_vec, scaled, inverse):
    grad_scaled = grad_norm * gain_vec
    first_mean = jnp.mean(grad_scaled, axis=-1, keepdims=True)
    second_mean = jnp.mean(grad_scaled * scaled, axis=-1, keepdims=True)
    return (grad_scaled - first_mean - scaled * second_mean) * inverse


def to_channels(tile):
    t, rows, cols, chans = tile.shape
    wide = lax.all_to_all(tile, "col", split_axis=3, concat_axis=2, tiled=True)
    own = wide.shape[3]
    parts = lax.axis_size("row")
    halves = parts // own
    split = wide.reshape(t, rows, halves, wide.shape[2] // halves, own)
    split = jnp.transpose(split, (4, 2, 0, 1, 3)).reshape(parts, t, rows, -1)
    moved = lax.all_to_all(split, "row", split_axis=0, concat_axis=0, tiled=True)
    return jnp.transpose(moved, (1, 0, 2, 3)).reshape(t, parts * rows, -1)


def from_channels(whole, own):
    parts = lax.axis_size("row")
    halves = parts // own
    t, all_rows, wide = whole.shape
    rows = all_rows // parts
    split = jnp.transpose(whole.reshape(t, parts, rows, wide), (1, 0, 2, 3))
    moved = lax.all_to_all(split, "row", split_axis=0, concat_axis=0, tiled=True)
    moved = moved.reshape(own, halves, t, rows, wide)
    moved = jnp.transpose(moved, (2, 3, 1, 4, 0)).reshape(t, rows, halves * wide, own)
    return lax.all_to_all(moved, "col", split_axis=2, concat_axis=3, tiled=True)


def per_device(
    pair, residue_mask, cotangent, w_in, w_out, w_gout, gain_in, bias_in, gain_out, bias_out
):
    hidden = w_out.shape[0]
    row_tile = pair.shape[0]
    col_tile = pair.shape[1]
    rows = lax.axis_size("row")
    own = hidden // lax.axis_size("col")
    row_index = lax.axis_index("row")
    col_index = lax.axis_index("col")
    valid = residue_mask.astype(jnp.float32)
    row_valid = lax.dynamic_slice_in_dim(valid, row_index * row_tile, row_tile)
    col_valid = lax.dynamic_slice_in_dim(valid, col_index * col_tile, col_tile)
    pair_mask = (row_valid[:, None] * col_valid[None, :])[..., None]
    normed, scaled_in, inverse_in = normalize(pair.astype(jnp.float32), gain_in, bias_in)
    normed = normed.astype(jnp.bfloat16)
    mixed = jnp.dot(normed, w_in, preferred_element_type=jnp.float32)
    projected = mixed[..., : 2 * hidden]
    gates = jax.nn.sigmoid(mixed[..., 2 * hidden :])
    branch = (gates * projected * pair_mask).astype(jnp.bfloat16)
    both = to_channels(jnp.stack([branch[..., :hidden], branch[..., hidden:]]))
    left, right = both[0], both[1]
    half = row_index % 2
    swap = [(r, r ^ 1) for r in range(rows)]
    tri_all = jnp.einsum("ik,jk->ij", left, right, preferred_element_type=jnp.float32)
    width = tri_all.shape[1] // 2
    mine = lax.dynamic_slice_in_dim(tri_all, half * width, width, axis=1)
    theirs = lax.dynamic_slice_in_dim(tri_all, (1 - half) * width, width, axis=1)
    tri_half = mine + lax.ppermute(theirs, "row", swap)
    tri = from_channels(tri_half.astype(jnp.bfloat16)[None], own)[0].astype(jnp.float32)
    out_norm, scaled_out, inverse_out = normalize(tri, gain_out, bias_out)
    out_norm = out_norm.astype(jnp.bfloat16)
    outer_gate = jax.nn.sigmoid(jnp.dot(normed, w_gout, preferred_element_type=jnp.float32))
    outer_proj = jnp.dot(out_norm, w_out, preferred_element_type=jnp.float32)
    output = (outer_gate * outer_proj).astype(jnp.bfloat16)
    upstream = cotangent.astype(jnp.float32)
    grad_proj = (upstream * outer_gate).astype(jnp.bfloat16)
    grad_gate = (upstream * outer_proj * outer_gate * (1.0 - outer_gate)).astype(jnp.bfloat16)
    grad_outnorm = jnp.dot(grad_proj, w_out.T, preferred_element_type=jnp.float32)
    grad_tri = norm_back(grad_outnorm, gain_out, scaled_out, inverse_out).astype(jnp.bfloat16)
    grad_half = to_channels(grad_tri[None])[0]
    other = lax.ppermute(grad_half, "row", swap)
    first = jnp.where(half == 0, grad_half, other)
    second = jnp.where(half == 0, other, grad_half)
    grad_all = jnp.concatenate([first, second], axis=1)
    grad_left = jnp.einsum("ij,jk->ik", grad_all, right, preferred_element_type=jnp.float32)
    grad_right = jnp.einsum("ij,ik->jk", grad_all, left, preferred_element_type=jnp.float32)
    grads = from_channels(jnp.stack([grad_left, grad_right]).astype(jnp.bfloat16), own)
    grads = grads.astype(jnp.float32)
    grad_branch = jnp.concatenate([grads[0], grads[1]], axis=-1) * pair_mask
    grad_mixed = jnp.concatenate(
        [grad_branch * gates, grad_branch * projected * gates * (1.0 - gates)], axis=-1
    ).astype(jnp.bfloat16)
    grad_normed = jnp.dot(grad_mixed, w_in.T, preferred_element_type=jnp.float32) + jnp.dot(
        grad_gate, w_gout.T, preferred_element_type=jnp.float32
    )
    grad_pair = norm_back(grad_normed, gain_in, scaled_in, inverse_in).astype(jnp.bfloat16)
    return (output, grad_pair)


def solution(mesh):
    return jax.shard_map(
        per_device,
        mesh=mesh,
        in_specs=(
            P("row", "col", None),
            P(),
            P("row", "col", None),
            P(),
            P(),
            P(),
            P(),
            P(),
            P(),
            P(),
        ),
        out_specs=(P("row", "col", None), P("row", "col", None)),
        check_vma=False,
    )
```

```python
import jax
import jax.numpy as jnp
from jax import lax
from jax.experimental import pallas as pl
from jax.experimental.pallas import tpu as pltpu
from jax.sharding import PartitionSpec as P

epsilon = 1e-05
MESH = pl.DeviceIdType.MESH
F32 = jnp.float32
BF16 = jnp.bfloat16

PLANE = 16
DEPTH = 8
U = 8
G = 4
TILE = 32
LANES = 128
CHAN = 128
WIDE = 256


def dot(a, b):
    return lax.dot_general(a, b, (((1,), (0,)), ((), ())), preferred_element_type=F32)


def dot_nt(a, b):
    return lax.dot_general(a, b, (((1,), (1,)), ((), ())), preferred_element_type=F32)


def dot_tn(a, b):
    return lax.dot_general(a, b, (((0,), (0,)), ((), ())), preferred_element_type=F32)


def swap_groups(parts, lane):
    low = lane < 64
    even = (lane // 32) % 2 == 0
    half = [[None, None], [None, None]]
    for bit in range(2):
        a, b = parts[bit], parts[2 + bit]
        half[0][bit] = jnp.where(low, a, pltpu.roll(b, 64, 1))
        half[1][bit] = jnp.where(low, pltpu.roll(a, 64, 1), b)
    out = []
    for bit in range(2):
        a, b = half[bit]
        out.append(jnp.where(even, a, pltpu.roll(b, 32, 1)))
        out.append(jnp.where(even, pltpu.roll(a, 96, 1), b))
    return out


def plane_index(x_hi, zh, p):
    return x_hi * 8 + ((p % 2) * 2 + zh) * 2 + p // 2


def kernel(
    pair_ref, mask_ref, cot_ref, w_in_ref, w_out_ref, w_gout_ref,
    gain_in_ref, bias_in_ref, gain_out_ref, bias_out_ref,
    out_ref, grad_ref,
    w_in_t, w_out_t, w_gout_t, masks, normed_s, scaled_s, inv_s,
    proj_s, gate_s, ogate_s, cot_s, oproj_s, ggate_s,
    stage,
    ps, pr, zs, zr, us, ur,
    swap_s, swap_r, gother,
    psend, precv, zsend, zrecv, csend, crecv,
):
    row = lax.axis_index("row")
    col = lax.axis_index("col")
    z = row % 8
    x_hi = row // 8
    core = col % 2
    me = x_hi * 8 + col // 2

    def plane_peer(d):
        peer = (me + d) % PLANE
        return peer, ((peer // 8) * 8 + z, (peer % 8) * 2 + core)

    def depth_peer(d):
        peer = (z + d) % DEPTH
        return peer, (x_hi * 8 + peer, col)

    partner = (row, col + 1 - 2 * core)

    barrier = pltpu.get_barrier_semaphore()

    @pl.loop(1, PLANE)
    def _(d):
        pl.semaphore_signal(barrier, inc=1, device_id=plane_peer(d)[1], device_id_type=MESH)

    @pl.loop(1, DEPTH)
    def _(d):
        pl.semaphore_signal(barrier, inc=1, device_id=depth_peer(d)[1], device_id_type=MESH)

    pl.semaphore_signal(barrier, inc=1, device_id=partner, device_id_type=MESH)

    def rows64(index):
        return pl.ds(pl.multiple_of(index * 64, 64), 64)

    def plane_copy(t, d):
        peer, where = plane_peer(d)
        return pltpu.make_async_remote_copy(
            src_ref=ps.at[t, rows64(peer)],
            dst_ref=pr.at[t, rows64(me)],
            send_sem=psend.at[t, d],
            recv_sem=precv.at[t, d],
            device_id=where,
            device_id_type=MESH,
        )

    def depth_copy(t, d, split):
        peer, where = depth_peer(d)
        if t == 1:
            source, target = peer, (z % 2) * 4 + z // 2
        elif t == 5:
            source, target = (peer % 2) * 4 + peer // 2, z
        else:
            source, target = peer, z
        return pltpu.make_async_remote_copy(
            src_ref=zs.at[t, source],
            dst_ref=zr.at[t, target],
            send_sem=zsend.at[t, d],
            recv_sem=zrecv.at[t, d],
            device_id=where,
            device_id_type=MESH,
        )

    def plane_start(t):
        pr[t, rows64(me), :] = ps[t, rows64(me), :]

        @pl.loop(1, PLANE)
        def _(d):
            plane_copy(t, d).start()

    def plane_wait(t):
        @pl.loop(1, PLANE)
        def _(d):
            plane_copy(t, d).wait_recv()

    def depth_start(t):
        order = (z % 2) * 4 + z // 2
        if t == 1:
            zr[t, order] = zs[t, z]
        elif t == 5:
            zr[t, z] = zs[t, order]
        else:
            zr[t, z] = zs[t, z]

        @pl.loop(1, DEPTH)
        def _(d):
            depth_copy(t, d, False).start()

    def depth_wait(t):
        @pl.loop(1, DEPTH)
        def _(d):
            depth_copy(t, d, False).wait_recv()

    lane = lax.broadcasted_iota(jnp.int32, (64, LANES), 1)

    def gather_tiles(t):
        for xh in range(2):
            for zh in range(2):
                parts = [
                    pr[t, plane_index(xh, zh, p) * 64 : plane_index(xh, zh, p) * 64 + 64, :].astype(F32)
                    for p in range(4)
                ]
                moved = swap_groups(parts, lane)
                whole = jnp.concatenate([m.reshape(8, 1, U, LANES) for m in moved], axis=1)
                zs[t, :, xh * 32 : xh * 32 + 32, zh * 128 : zh * 128 + 128] = whole.reshape(
                    8, 32, LANES
                ).astype(BF16)

    def scatter_tiles(t):
        for xh in range(2):
            for zh in range(2):
                block = zr[t, :, xh * 32 : xh * 32 + 32, zh * 128 : zh * 128 + 128]
                block = block.astype(F32).reshape(8, G, U, LANES)
                parts = [block[:, g].reshape(64, LANES) for g in range(G)]
                moved = swap_groups(parts, lane)
                for p in range(4):
                    at = plane_index(xh, zh, p) * 64
                    ps[t, at : at + 64, :] = moved[p].astype(BF16)

    def strided(u):
        return pl.ds(u, CHAN, stride=U)

    w_in_t[...] = w_in_ref[...].astype(F32).T.astype(BF16)
    w_out_t[...] = w_out_ref[...].astype(F32).T.astype(BF16)
    w_gout_t[...] = w_gout_ref[...].astype(F32).T.astype(BF16)

    def column(ref):
        return jnp.broadcast_to(ref[...].reshape(1, CHAN), (8, CHAN)).T[:, 0:1]

    gain_in = column(gain_in_ref)
    bias_in = column(bias_in_ref)
    gain_out = column(gain_out_ref)
    bias_out = column(bias_out_ref)

    valid = jnp.broadcast_to(mask_ref[...].reshape(1, 512), (8, 512)).astype(F32).astype(BF16)
    number = lax.broadcasted_iota(jnp.int32, (512, LANES), 0)
    place = lax.broadcasted_iota(jnp.int32, (512, LANES), 1)
    col_pick = (number == col * TILE + place % 32).astype(F32).astype(BF16)
    col_valid = dot(valid, col_pick)

    def normalize(values, gain, bias):
        average = jnp.mean(values, axis=0, keepdims=True)
        centred = values - average
        inverse = lax.rsqrt(jnp.mean(centred * centred, axis=0, keepdims=True) + epsilon)
        scaled = centred * inverse
        return scaled * gain + bias, scaled, inverse

    def norm_back(grad, gain, scaled, inverse):
        s = grad * gain
        first = jnp.mean(s, axis=0, keepdims=True)
        second = jnp.mean(s * scaled, axis=0, keepdims=True)
        return (s - first - scaled * second) * inverse

    def tile_of(ref, u):
        rows = jnp.concatenate([ref[g * U + u] for g in range(G)], axis=0)
        return rows.astype(F32).T

    def branch(t, u, normed):
        base = t * CHAN
        projected = dot(w_in_t[base : base + CHAN, :], normed)
        gates = jax.nn.sigmoid(dot(w_in_t[2 * CHAN + base : 3 * CHAN + base, :], normed))
        mask = masks[u]
        gate_s[u, base : base + CHAN, :] = gates * mask
        value = gates * projected * mask
        proj_s[u, base : base + CHAN, :] = value * (1.0 - gates)
        stage[t, strided(u), :] = value

    @pl.loop(0, U)
    def _(u):
        row_pick = (number == row * TILE + (place // 32) * U + u).astype(F32).astype(BF16)
        masks[u] = (dot(valid, row_pick) * col_valid)[0:1, :]
        normed, scaled, inverse = normalize(tile_of(pair_ref, u), gain_in, bias_in)
        normed = normed.astype(BF16)
        normed_s[u] = normed
        scaled_s[u] = scaled
        inv_s[u] = inverse
        branch(0, u, normed)

    ps[0] = stage[0].astype(BF16)
    pl.semaphore_wait(barrier, (PLANE - 1) + (DEPTH - 1) + 1)
    plane_start(0)

    @pl.loop(0, U)
    def _(u):
        branch(1, u, normed_s[u])

    ps[1] = stage[1].astype(BF16)
    plane_start(1)

    plane_wait(0)
    gather_tiles(0)
    depth_start(0)
    plane_wait(1)
    gather_tiles(1)
    depth_start(1)

    @pl.loop(0, U)
    def _(u):
        ogate_s[u] = jax.nn.sigmoid(dot(w_gout_t[...], normed_s[u]))
        cot_s[u] = tile_of(cot_ref, u)

    depth_wait(0)
    depth_wait(1)

    left = zr[0].reshape(8 * 64, WIDE)

    def right_half(which):
        return zr[1, pl.ds(which * 4, 4)].reshape(WIDE, WIDE)

    def to_partner(i, src, dst):
        return pltpu.make_async_remote_copy(
            src_ref=src,
            dst_ref=dst,
            send_sem=csend.at[i],
            recv_sem=crecv.at[i],
            device_id=partner,
            device_id_type=MESH,
        )

    swap_s[...] = dot_nt(left, right_half(1 - core)).astype(BF16)
    tri_copy = to_partner(0, swap_s, swap_r)
    tri_copy.start()
    mine = dot_nt(left, right_half(core))
    tri_copy.wait_recv()
    zs[2] = (mine + swap_r[...].astype(F32)).astype(BF16).reshape(8, 64, WIDE)
    depth_start(2)
    depth_wait(2)
    scatter_tiles(2)
    plane_start(2)
    plane_wait(2)

    stage[2] = pr[2].astype(F32)

    @pl.loop(0, U)
    def _(u):
        tri = stage[2, strided(u), :]
        out_norm, scaled, inverse = normalize(tri, gain_out, bias_out)
        outer_proj = dot(w_out_t[...], out_norm.astype(BF16))
        outer_gate = ogate_s[u]
        upstream = cot_s[u]
        gated = upstream * outer_gate
        grad_outnorm = dot(w_out_ref[...], gated.astype(BF16))
        oproj_s[u] = outer_proj
        stage[3, strided(u), :] = norm_back(grad_outnorm, gain_out, scaled, inverse)

    ps[3] = stage[3].astype(BF16)
    plane_start(3)

    @pl.loop(0, U)
    def _(u):
        outer_proj = oproj_s[u]
        outer_gate = ogate_s[u]
        whole = (outer_gate * outer_proj).T.astype(BF16)
        for g in range(G):
            out_ref[g * U + u] = whole[g * TILE : g * TILE + TILE, :]
        grad_gate = (cot_s[u] * outer_proj * outer_gate * (1.0 - outer_gate)).astype(BF16)
        ggate_s[u] = dot(w_gout_ref[...], grad_gate)

    plane_wait(3)
    gather_tiles(3)
    depth_start(3)
    depth_wait(3)

    grad_copy = to_partner(1, zr.at[3], gother)
    grad_copy.start()
    own = zr[3].reshape(512, WIDE)
    half = dot_tn(own, left).astype(BF16).reshape(4, 64, WIDE)
    zs[5, pl.ds(core * 4, 4)] = half
    grad_left = dot(own, right_half(core))
    grad_copy.wait_recv()
    other = gother[...].reshape(512, WIDE)
    grad_left = grad_left + dot(other, right_half(1 - core))
    zs[4] = grad_left.astype(BF16).reshape(8, 64, WIDE)
    depth_start(4)
    half = dot_tn(other, left).astype(BF16).reshape(4, 64, WIDE)
    zs[5, pl.ds((1 - core) * 4, 4)] = half
    depth_start(5)
    depth_wait(4)
    scatter_tiles(4)
    plane_start(4)
    depth_wait(5)
    scatter_tiles(5)
    plane_start(5)
    plane_wait(4)
    stage[4] = pr[4].astype(F32)
    plane_wait(5)
    stage[5] = pr[5].astype(F32)

    @pl.loop(0, U)
    def _(u):
        gl = stage[4, strided(u), :]
        gr = stage[5, strided(u), :]
        mixed = jnp.concatenate(
            [
                gl * gate_s[u, 0:CHAN, :],
                gr * gate_s[u, CHAN : 2 * CHAN, :],
                gl * proj_s[u, 0:CHAN, :],
                gr * proj_s[u, CHAN : 2 * CHAN, :],
            ],
            axis=0,
        ).astype(BF16)
        grad_normed = dot(w_in_ref[...], mixed) + ggate_s[u]
        whole = norm_back(grad_normed, gain_in, scaled_s[u], inv_s[u]).T.astype(BF16)
        for g in range(G):
            grad_ref[g * U + u] = whole[g * TILE : g * TILE + TILE, :]

    for t in range(6):

        @pl.loop(1, PLANE)
        def _(d):
            plane_copy(t, d).wait_send()

        @pl.loop(1, DEPTH)
        def _(d):
            depth_copy(t, d, False).wait_send()

    tri_copy.wait_send()
    grad_copy.wait_send()


def per_device(
    pair, residue_mask, cotangent, w_in, w_out, w_gout, gain_in, bias_in, gain_out, bias_out
):
    vmem = pl.BlockSpec(memory_space=pltpu.VMEM)
    shape = jax.ShapeDtypeStruct(pair.shape, BF16)
    return pl.pallas_call(
        kernel,
        out_shape=(shape, shape),
        in_specs=[vmem] * 10,
        out_specs=(vmem, vmem),
        scratch_shapes=[
            pltpu.VMEM((4 * CHAN, CHAN), BF16),
            pltpu.VMEM((CHAN, CHAN), BF16),
            pltpu.VMEM((CHAN, CHAN), BF16),
            pltpu.VMEM((U, 1, LANES), F32),
            pltpu.VMEM((U, CHAN, LANES), BF16),
            pltpu.VMEM((U, CHAN, LANES), F32),
            pltpu.VMEM((U, 1, LANES), F32),
            pltpu.VMEM((U, 2 * CHAN, LANES), F32),
            pltpu.VMEM((U, 2 * CHAN, LANES), F32),
            pltpu.VMEM((U, CHAN, LANES), F32),
            pltpu.VMEM((U, CHAN, LANES), F32),
            pltpu.VMEM((U, CHAN, LANES), F32),
            pltpu.VMEM((U, CHAN, LANES), F32),
            pltpu.VMEM((6, CHAN * U, LANES), F32),
            pltpu.VMEM((6, CHAN * U, LANES), BF16),
            pltpu.VMEM((6, CHAN * U, LANES), BF16),
            pltpu.VMEM((6, DEPTH, 64, WIDE), BF16),
            pltpu.VMEM((6, DEPTH, 64, WIDE), BF16),
            pltpu.VMEM((8, LANES), F32),
            pltpu.VMEM((8, LANES), F32),
            pltpu.VMEM((512, WIDE), BF16),
            pltpu.VMEM((512, WIDE), BF16),
            pltpu.VMEM((DEPTH, 64, WIDE), BF16),
            pltpu.SemaphoreType.DMA((6, PLANE)),
            pltpu.SemaphoreType.DMA((6, PLANE)),
            pltpu.SemaphoreType.DMA((6, DEPTH)),
            pltpu.SemaphoreType.DMA((6, DEPTH)),
            pltpu.SemaphoreType.DMA((2,)),
            pltpu.SemaphoreType.DMA((2,)),
        ],
        compiler_params=pltpu.CompilerParams(
            collective_id=0, has_side_effects=True, vmem_limit_bytes=48 * 1024 * 1024
        ),
    )(pair, residue_mask, cotangent, w_in, w_out, w_gout, gain_in, bias_in, gain_out, bias_out)


def solution(mesh):
    tile = P("row", "col", None)
    return jax.shard_map(
        per_device,
        mesh=mesh,
        in_specs=(tile, P(), tile, P(), P(), P(), P(), P(), P(), P()),
        out_specs=(tile, tile),
        check_vma=False,
    )
```

```python
import jax
import jax.numpy as jnp
from jax import lax
from jax.experimental import pallas as pl
from jax.experimental.pallas import tpu as pltpu
from jax.sharding import PartitionSpec as P

epsilon = 1e-05
MESH = pl.DeviceIdType.MESH
F32 = jnp.float32
BF16 = jnp.bfloat16

U = 8
G = 4
V = 4
TILE = 32
LANES = 128
CHAN = 128
WIDE = 256
Q = 8


def dot(a, b):
    return lax.dot_general(a, b, (((1,), (0,)), ((), ())), preferred_element_type=F32)


def dot_nt(a, b):
    return lax.dot_general(a, b, (((1,), (1,)), ((), ())), preferred_element_type=F32)


def dot_tn(a, b):
    return lax.dot_general(a, b, (((0,), (0,)), ((), ())), preferred_element_type=F32)


def swap_groups(parts):
    lane = lax.broadcasted_iota(jnp.int32, parts[0].shape, 1)
    low = lane < 64
    even = (lane // 32) % 2 == 0
    half = [[None, None], [None, None]]
    for bit in range(2):
        a, b = parts[bit], parts[2 + bit]
        half[0][bit] = jnp.where(low, a, pltpu.roll(b, 64, 1))
        half[1][bit] = jnp.where(low, pltpu.roll(a, 64, 1), b)
    out = []
    for bit in range(2):
        a, b = half[bit]
        out.append(jnp.where(even, a, pltpu.roll(b, 32, 1)))
        out.append(jnp.where(even, pltpu.roll(a, 96, 1), b))
    return out


def normalize(values, gain, bias):
    average = jnp.mean(values, axis=0, keepdims=True)
    centred = values - average
    inverse = lax.rsqrt(jnp.mean(centred * centred, axis=0, keepdims=True) + epsilon)
    scaled = centred * inverse
    return scaled * gain + bias, scaled, inverse


def norm_back(grad, gain, scaled, inverse):
    s = grad * gain
    first = jnp.mean(s, axis=0, keepdims=True)
    second = jnp.mean(s * scaled, axis=0, keepdims=True)
    return (s - first - scaled * second) * inverse


def tile_of(ref, v):
    rows = [ref[g * U + 2 * v + e] for e in range(2) for g in range(G)]
    return jnp.concatenate(rows, axis=0).astype(F32).T


def store_tile(ref, v, values):
    whole = values.T.astype(BF16)
    for e in range(2):
        for g in range(G):
            at = (e * G + g) * TILE
            ref[g * U + 2 * v + e] = whole[at : at + TILE, :]


def kernel(
    pair_hbm, mask_hbm, cot_hbm, w_in_hbm, w_out_hbm, w_gout_hbm,
    gain_in_hbm, bias_in_hbm, gain_out_hbm, bias_out_hbm,
    out_hbm, grad_hbm,
    pair_ref, mask_ref, cot_ref, w_in_ref, w_out_ref, w_gout_ref,
    gain_in_ref, bias_in_ref, gain_out_ref, bias_out_ref,
    out_ref, grad_ref,
    w_in_t, w_out_t, w_gout_t, masks, normed_s, scaled_s, inv_s,
    proj_s, gate_s, ogate_s, cot_s, oproj_s, ggate_s,
    stage, sx, rx, left_m, right_m, own_m, other_m, swap_s, swap_r,
    send_sem, recv_sem, csend, crecv, local_sem, ready_sem,
):
    arrays = [
        (pair_hbm, pair_ref), (mask_hbm, mask_ref), (w_in_hbm, w_in_ref), (w_out_hbm, w_out_ref),
        (w_gout_hbm, w_gout_ref), (gain_in_hbm, gain_in_ref), (bias_in_hbm, bias_in_ref),
        (gain_out_hbm, gain_out_ref), (bias_out_hbm, bias_out_ref), (cot_hbm, cot_ref),
    ]
    loads = [
        pltpu.make_async_copy(src, dst, local_sem.at[i]) for i, (src, dst) in enumerate(arrays)
    ]
    for load in loads:
        load.start()
    store_out = pltpu.make_async_copy(out_ref, out_hbm, local_sem.at[10])
    store_grad = pltpu.make_async_copy(grad_ref, grad_hbm, local_sem.at[11])

    row = lax.axis_index("row")
    col = lax.axis_index("col")
    z = row % 8
    x_hi = row // 8
    core = col % 2
    q = col // 2
    partner = (row, col + 1 - 2 * core)

    barrier = pltpu.get_barrier_semaphore()

    def depth_peer(d):
        return (x_hi * 8 + (z + d) % 8, col)

    @pl.loop(1, 16)
    def _(d):
        peer = (x_hi * 8 + q + d) % 16
        where = ((peer // 8) * 8 + z, (peer % 8) * 2 + core)
        pl.semaphore_signal(barrier, inc=1, device_id=where, device_id_type=MESH)

    @pl.loop(1, 8)
    def _(d):
        pl.semaphore_signal(barrier, inc=1, device_id=depth_peer(d), device_id_type=MESH)

    pl.semaphore_signal(barrier, inc=1, device_id=partner, device_id_type=MESH)

    def post(t, to_row, to_q):
        return pltpu.make_async_remote_copy(
            src_ref=sx.at[t, to_row // 2, to_row % 2, to_q],
            dst_ref=rx.at[t, row // 2, row % 2, q],
            send_sem=send_sem.at[t],
            recv_sem=recv_sem.at[t],
            device_id=(to_row, to_q * 2 + core),
            device_id_type=MESH,
        )

    def keep(t):
        pltpu.make_async_copy(
            sx.at[t, row // 2, row % 2, q], rx.at[t, row // 2, row % 2, q], recv_sem.at[t]
        ).start()

    def send(t):
        keep(t)

        @pl.loop(1, 128)
        def _(d):
            to = (row * 8 + q + d) % 128
            post(t, to // 8, to % 8).start()

    def send_rows(t, parity):
        same = row % 2 == parity

        @pl.when(same)
        def _():
            keep(t)

        @pl.when(jnp.logical_not(same))
        def _():
            post(t, (row // 2) * 2 + parity, q).start()

        @pl.loop(1, 64)
        def _(d):
            to = ((row // 2) * 8 + q + d) % 64
            post(t, (to // 8) * 2 + parity, to % 8).start()

    def receive(t):
        pltpu.make_async_copy(sx.at[t], rx.at[t], recv_sem.at[t]).wait()

    def sent(t):
        for part in (sx.at[t, pl.ds(0, 7)], sx.at[t, 7, 0], sx.at[t, 7, 1, pl.ds(0, 7)]):
            pltpu.make_async_copy(part, part, send_sem.at[t]).wait()

    def gather(t, half):
        parts = [rx[t, :, :, half * 4 + p].astype(F32).reshape(16 * U, LANES) for p in range(4)]
        moved = [m.reshape(16, 1, U, LANES) for m in swap_groups(parts)]
        return jnp.concatenate(moved, axis=1).reshape(512, LANES).astype(BF16)

    def scatter(t, block, half, parity=None):
        rows = block.shape[0] // TILE
        block = block.reshape(rows, G, U, LANES)
        parts = [block[:, g].reshape(rows * U, LANES) for g in range(G)]
        for p, moved in enumerate(swap_groups(parts)):
            if parity is None:
                sx[t, :, :, half * 4 + p] = moved.reshape(8, 2, U, LANES).astype(BF16)
            else:
                sx[t, :, parity, half * 4 + p] = moved.reshape(8, U, LANES).astype(BF16)

    def halves(x):
        return [x[:, 0:LANES], x[:, LANES : 2 * LANES]]

    def strided(v, e):
        return pl.ds(2 * v + e, CHAN, stride=U)

    def put(t, v, values):
        for e, value in enumerate(halves(values)):
            stage[t, strided(v, e), :] = value

    def get(t, v):
        return jnp.concatenate([stage[t, strided(v, e), :] for e in range(2)], axis=1)

    def pack(t):
        sx[t] = stage[t].reshape(8, 2, Q, U, LANES).astype(BF16)

    def unpack(t):
        stage[t] = rx[t].astype(F32).reshape(CHAN * U, LANES)

    for load in loads[1:9]:
        load.wait()
    w_in_t[...] = w_in_ref[...].astype(F32).T.astype(BF16)
    w_out_t[...] = w_out_ref[...].astype(F32).T.astype(BF16)
    w_gout_t[...] = w_gout_ref[...].astype(F32).T.astype(BF16)

    def column(ref):
        return jnp.broadcast_to(ref[...].reshape(1, CHAN), (8, CHAN)).T[:, 0:1]

    gain_in = column(gain_in_ref)
    bias_in = column(bias_in_ref)
    gain_out = column(gain_out_ref)
    bias_out = column(bias_out_ref)

    valid = jnp.broadcast_to(mask_ref[...].reshape(1, 512), (8, 512)).astype(F32).astype(BF16)
    number = lax.broadcasted_iota(jnp.int32, (512, WIDE), 0)
    place = lax.broadcasted_iota(jnp.int32, (512, WIDE), 1)
    col_pick = (number == col * TILE + place % 32).astype(F32).astype(BF16)
    col_valid = dot(valid, col_pick)
    for v in range(V):
        first = row * TILE + ((place // 32) % G) * U + place // LANES + 2 * v
        row_pick = (number == first).astype(F32).astype(BF16)
        masks[v] = (dot(valid, row_pick) * col_valid)[0:1, :]

    def branch(t, v, normed):
        base = t * CHAN
        projected = dot(w_in_t[base : base + CHAN, :], normed)
        gates = jax.nn.sigmoid(dot(w_in_t[2 * CHAN + base : 3 * CHAN + base, :], normed))
        mask = masks[v]
        gate_s[v, base : base + CHAN, :] = gates * mask
        value = gates * projected * mask
        proj_s[v, base : base + CHAN, :] = value * (1.0 - gates)
        put(t, v, value)

    loads[0].wait()

    @pl.loop(0, V)
    def _(v):
        normed, scaled, inverse = normalize(tile_of(pair_ref, v), gain_in, bias_in)
        normed = normed.astype(BF16)
        normed_s[v] = normed
        scaled_s[v] = scaled
        inv_s[v] = inverse
        branch(1, v, normed)

    pack(1)
    pl.semaphore_wait(barrier, 15 + 7 + 1)

    @pl.loop(1, 8)
    def _(d):
        pl.semaphore_signal(ready_sem, inc=1, device_id=depth_peer(d), device_id_type=MESH)

    pl.semaphore_wait(ready_sem, 7)
    send(1)

    @pl.loop(0, V)
    def _(v):
        branch(0, v, normed_s[v])

    pack(0)
    send(0)

    loads[9].wait()

    @pl.loop(0, V)
    def _(v):
        ogate_s[v] = jax.nn.sigmoid(dot(w_gout_t[...], normed_s[v]))
        cot_s[v] = tile_of(cot_ref, v)

    receive(1)
    for half in range(2):
        whole = gather(1, half).reshape(8, 2, TILE, LANES)
        for side in range(2):
            right_m[side, :, half * LANES : half * LANES + LANES] = whole[:, side].reshape(WIDE, LANES)

    receive(0)
    for half in range(2):
        left_m[:, half * LANES : half * LANES + LANES] = gather(0, half)

    def to_partner(i, src, dst):
        return pltpu.make_async_remote_copy(
            src_ref=src,
            dst_ref=dst,
            send_sem=csend.at[i],
            recv_sem=crecv.at[i],
            device_id=partner,
            device_id_type=MESH,
        )

    swap_s[...] = dot_nt(left_m[...], right_m[1 - core]).astype(BF16)
    tri_copy = to_partner(0, swap_s, swap_r)
    tri_copy.start()
    mine = dot_nt(left_m[...], right_m[core])
    tri_copy.wait_recv()
    mine = mine + swap_r[...].astype(F32)
    for half in range(2):
        scatter(2, halves(mine)[half], half)
    send(2)
    receive(2)

    unpack(2)

    @pl.loop(0, V)
    def _(v):
        out_norm, scaled, inverse = normalize(get(2, v), gain_out, bias_out)
        outer_proj = dot(w_out_t[...], out_norm.astype(BF16))
        gated = cot_s[v] * ogate_s[v]
        grad_outnorm = dot(w_out_ref[...], gated.astype(BF16))
        oproj_s[v] = outer_proj
        put(3, v, norm_back(grad_outnorm, gain_out, scaled, inverse))

    pack(3)
    send(3)

    @pl.loop(0, V)
    def _(v):
        outer_proj = oproj_s[v]
        outer_gate = ogate_s[v]
        store_tile(out_ref, v, outer_gate * outer_proj)
        grad_gate = (cot_s[v] * outer_proj * outer_gate * (1.0 - outer_gate)).astype(BF16)
        ggate_s[v] = dot(w_gout_ref[...], grad_gate)

    store_out.start()
    receive(3)

    for half in range(2):
        own_m[:, half * LANES : half * LANES + LANES] = gather(3, half)
    grad_copy = to_partner(1, own_m, other_m)
    grad_copy.start()
    grad_right = dot_tn(own_m[...], left_m[...])
    for half in range(2):
        scatter(5, halves(grad_right)[half], half, core)
    send_rows(5, core)
    grad_left = dot(own_m[...], right_m[core])
    grad_copy.wait_recv()
    grad_left = grad_left + dot(other_m[...], right_m[1 - core])
    for half in range(2):
        scatter(4, halves(grad_left)[half], half)
    send(4)
    grad_right = dot_tn(other_m[...], left_m[...])
    for half in range(2):
        scatter(5, halves(grad_right)[half], half, 1 - core)
    send_rows(5, 1 - core)
    receive(4)
    unpack(4)
    receive(5)
    unpack(5)

    @pl.loop(0, V)
    def _(v):
        gl = get(4, v)
        gr = get(5, v)
        mixed = jnp.concatenate(
            [
                gl * gate_s[v, 0:CHAN, :],
                gr * gate_s[v, CHAN : 2 * CHAN, :],
                gl * proj_s[v, 0:CHAN, :],
                gr * proj_s[v, CHAN : 2 * CHAN, :],
            ],
            axis=0,
        ).astype(BF16)
        grad_normed = dot(w_in_ref[...], mixed) + ggate_s[v]
        store_tile(grad_ref, v, norm_back(grad_normed, gain_in, scaled_s[v], inv_s[v]))

    store_grad.start()
    for t in range(6):
        sent(t)
    tri_copy.wait_send()
    grad_copy.wait_send()
    store_out.wait()
    store_grad.wait()


def per_device(
    pair, residue_mask, cotangent, w_in, w_out, w_gout, gain_in, bias_in, gain_out, bias_out
):
    hbm = pl.BlockSpec(memory_space=pl.ANY)
    shape = jax.ShapeDtypeStruct(pair.shape, BF16)
    args = (
        pair, residue_mask, cotangent, w_in, w_out, w_gout, gain_in, bias_in, gain_out, bias_out
    )
    return pl.pallas_call(
        kernel,
        out_shape=(shape, shape),
        in_specs=[hbm] * 10,
        out_specs=(hbm, hbm),
        scratch_shapes=[pltpu.VMEM(a.shape, a.dtype) for a in args]
        + [
            pltpu.VMEM(pair.shape, BF16),
            pltpu.VMEM(pair.shape, BF16),
            pltpu.VMEM((4 * CHAN, CHAN), BF16),
            pltpu.VMEM((CHAN, CHAN), BF16),
            pltpu.VMEM((CHAN, CHAN), BF16),
            pltpu.VMEM((V, 1, WIDE), F32),
            pltpu.VMEM((V, CHAN, WIDE), BF16),
            pltpu.VMEM((V, CHAN, WIDE), F32),
            pltpu.VMEM((V, 1, WIDE), F32),
            pltpu.VMEM((V, 2 * CHAN, WIDE), F32),
            pltpu.VMEM((V, 2 * CHAN, WIDE), F32),
            pltpu.VMEM((V, CHAN, WIDE), F32),
            pltpu.VMEM((V, CHAN, WIDE), F32),
            pltpu.VMEM((V, CHAN, WIDE), F32),
            pltpu.VMEM((V, CHAN, WIDE), F32),
            pltpu.VMEM((6, CHAN * U, LANES), F32),
            pltpu.VMEM((6, 8, 2, Q, U, LANES), BF16),
            pltpu.VMEM((6, 8, 2, Q, U, LANES), BF16),
            pltpu.VMEM((512, WIDE), BF16),
            pltpu.VMEM((2, WIDE, WIDE), BF16),
            pltpu.VMEM((512, WIDE), BF16),
            pltpu.VMEM((512, WIDE), BF16),
            pltpu.VMEM((512, WIDE), BF16),
            pltpu.VMEM((512, WIDE), BF16),
            pltpu.SemaphoreType.DMA((6,)),
            pltpu.SemaphoreType.DMA((6,)),
            pltpu.SemaphoreType.DMA((2,)),
            pltpu.SemaphoreType.DMA((2,)),
            pltpu.SemaphoreType.DMA((12,)),
            pltpu.SemaphoreType.REGULAR,
        ],
        compiler_params=pltpu.CompilerParams(
            collective_id=0, has_side_effects=True, vmem_limit_bytes=60 * 1024 * 1024
        ),
    )(*args)


def solution(mesh):
    tile = P("row", "col", None)
    return jax.shard_map(
        per_device,
        mesh=mesh,
        in_specs=(tile, P(), tile, P(), P(), P(), P(), P(), P(), P()),
        out_specs=(tile, tile),
        check_vma=False,
    )
```

```python
import jax
import jax.numpy as jnp
from jax import lax
from jax.experimental import pallas as pl
from jax.experimental.pallas import tpu as pltpu
from jax.sharding import PartitionSpec as P

epsilon = 1e-05
MESH = pl.DeviceIdType.MESH
F32 = jnp.float32
BF16 = jnp.bfloat16

U = 8
G = 4
V = 4
TILE = 32
LANES = 128
CHAN = 128
WIDE = 256


def dot(a, b):
    return lax.dot_general(a, b, (((1,), (0,)), ((), ())), preferred_element_type=F32)


def dot_nt(a, b):
    return lax.dot_general(a, b, (((1,), (1,)), ((), ())), preferred_element_type=F32)


def dot_tn(a, b):
    return lax.dot_general(a, b, (((0,), (0,)), ((), ())), preferred_element_type=F32)


def swap_groups(parts):
    lane = lax.broadcasted_iota(jnp.int32, parts[0].shape, 1)
    low = lane < 64
    even = (lane // 32) % 2 == 0
    half = [[None, None], [None, None]]
    for bit in range(2):
        a, b = parts[bit], parts[2 + bit]
        half[0][bit] = jnp.where(low, a, pltpu.roll(b, 64, 1))
        half[1][bit] = jnp.where(low, pltpu.roll(a, 64, 1), b)
    out = []
    for bit in range(2):
        a, b = half[bit]
        out.append(jnp.where(even, a, pltpu.roll(b, 32, 1)))
        out.append(jnp.where(even, pltpu.roll(a, 96, 1), b))
    return out


def normalize(values, gain, bias):
    average = jnp.mean(values, axis=0, keepdims=True)
    centred = values - average
    inverse = lax.rsqrt(jnp.mean(centred * centred, axis=0, keepdims=True) + epsilon)
    scaled = centred * inverse
    return scaled * gain + bias, scaled, inverse


def norm_back(grad, gain, scaled, inverse):
    s = grad * gain
    first = jnp.mean(s, axis=0, keepdims=True)
    second = jnp.mean(s * scaled, axis=0, keepdims=True)
    return (s - first - scaled * second) * inverse


def tile_of(ref, v):
    rows = [ref[g * U + 2 * v + e] for e in range(2) for g in range(G)]
    return jnp.concatenate(rows, axis=0).astype(F32).T


def store_tile(ref, v, values):
    whole = values.T.astype(BF16)
    for e in range(2):
        for g in range(G):
            at = (e * G + g) * TILE
            ref[g * U + 2 * v + e] = whole[at : at + TILE, :]


def kernel(
    pair_hbm, mask_hbm, cot_hbm, w_in_hbm, w_out_hbm, w_gout_hbm,
    gain_in_hbm, bias_in_hbm, gain_out_hbm, bias_out_hbm,
    out_ref, grad_ref,
    pair_ref, mask_ref, cot_ref, w_in_ref, w_out_ref, w_gout_ref,
    gain_in_ref, bias_in_ref, gain_out_ref, bias_out_ref,
    w_side, w_side_t, w_out_t, w_gout_t, masks, normed_s, scaled_s, inv_s,
    factor_s, ogate_s, cot_s, oproj_s, ggate_s,
    stage, tile_out, tile_in, owner_out, owner_in, left_m, right_m, grad_m, swap_s, swap_r,
    tile_send, tile_recv, owner_send, owner_recv, csend, crecv, local_sem, ready_sem,
):
    arrays = [
        (pair_hbm, pair_ref), (mask_hbm, mask_ref), (w_in_hbm, w_in_ref), (w_out_hbm, w_out_ref),
        (w_gout_hbm, w_gout_ref), (gain_in_hbm, gain_in_ref), (bias_in_hbm, bias_in_ref),
        (gain_out_hbm, gain_out_ref), (bias_out_hbm, bias_out_ref), (cot_hbm, cot_ref),
    ]
    loads = [
        pltpu.make_async_copy(src, dst, local_sem.at[i]) for i, (src, dst) in enumerate(arrays)
    ]
    for load in loads:
        load.start()

    row = lax.axis_index("row")
    col = lax.axis_index("col")
    z = row % 8
    x_hi = row // 8
    core = col % 2
    q = col // 2
    side = row % 2
    block = row // 2
    chan = row * 8 + q
    partner = (row, col + 1 - 2 * core)

    barrier = pltpu.get_barrier_semaphore()

    def plane_peer(d):
        peer = (x_hi * 8 + q + d) % 16
        return ((peer // 8) * 8 + z, (peer % 8) * 2 + core)

    @pl.loop(1, 16)
    def _(d):
        peer = (z * 2 + core + d) % 16
        where = (x_hi * 8 + peer // 2, q * 2 + peer % 2)
        pl.semaphore_signal(barrier, inc=1, device_id=where, device_id_type=MESH)

    @pl.loop(1, 16)
    def _(d):
        pl.semaphore_signal(barrier, inc=1, device_id=plane_peer(d), device_id_type=MESH)

    def to_owner(t, c):
        return pltpu.make_async_remote_copy(
            src_ref=tile_out.at[t, c],
            dst_ref=owner_in.at[t, block, col],
            send_sem=tile_send.at[t],
            recv_sem=owner_recv.at[t],
            device_id=(c // 8, (c % 8) * 2 + side),
            device_id_type=MESH,
        )

    def send_owners(t):
        @pl.when(side == core)
        def _():
            pltpu.make_async_copy(
                tile_out.at[t, chan], owner_in.at[t, block, col], owner_recv.at[t]
            ).start()

        @pl.when(side != core)
        def _():
            to_owner(t, chan).start()

        @pl.loop(1, 128)
        def _(d):
            to_owner(t, (chan + d) % 128).start()

    def to_tile(t, to_block, to_col):
        return pltpu.make_async_remote_copy(
            src_ref=owner_out.at[t, to_block, to_col],
            dst_ref=tile_in.at[t, chan],
            send_sem=owner_send.at[t],
            recv_sem=tile_recv.at[t],
            device_id=(to_block * 2 + core, to_col),
            device_id_type=MESH,
        )

    def send_tiles(t, half):
        own = jnp.logical_and(side == core, core == half)

        @pl.when(own)
        def _():
            pltpu.make_async_copy(
                owner_out.at[t, block, col], tile_in.at[t, chan], tile_recv.at[t]
            ).start()

        @pl.when(jnp.logical_not(own))
        def _():
            to_tile(t, block, q * 2 + half).start()

        @pl.loop(1, 64)
        def _(d):
            to = (block * 8 + q + d) % 64
            to_tile(t, to // 8, (to % 8) * 2 + half).start()

    def owner_receive(t):
        pltpu.make_async_copy(owner_out.at[t], owner_in.at[t], owner_recv.at[t]).wait()

    def tile_receive(t):
        pltpu.make_async_copy(tile_out.at[t], tile_in.at[t], tile_recv.at[t]).wait()

    def all_sent():
        for t in range(3):
            for ref, sem in ((tile_out.at[t], tile_send.at[t]), (owner_out.at[t], owner_send.at[t])):

                @pl.when(side != core)
                def _():
                    pltpu.make_async_copy(ref, ref, sem).wait()

            @pl.when(side == core)
            def _():
                ref = tile_out.at[t, pl.ds(0, 127)]
                pltpu.make_async_copy(ref, ref, tile_send.at[t]).wait()
                for part in (owner_out.at[t, pl.ds(0, 7)], owner_out.at[t, 7, pl.ds(0, 15)]):
                    pltpu.make_async_copy(part, part, owner_send.at[t]).wait()

    def gather(t):
        for at in range(4):
            parts = [
                owner_in[t, :, ((at % 2) * 4 + p) * 2 + at // 2].astype(F32).reshape(64, LANES)
                for p in range(4)
            ]
            moved = [m.reshape(8, 1, U, LANES) for m in swap_groups(parts)]
            yield at, jnp.concatenate(moved, axis=1).reshape(WIDE, LANES).astype(BF16)

    def scatter(t, half, values):
        for at in range(2):
            tiles = values[:, at * LANES : at * LANES + LANES].reshape(8, G, U, LANES)
            parts = [tiles[:, g].reshape(64, LANES) for g in range(G)]
            for p, moved in enumerate(swap_groups(parts)):
                owner_out[t, :, (at * 4 + p) * 2 + half] = moved.reshape(8, U, LANES).astype(BF16)

    def to_partner(i, src, dst):
        return pltpu.make_async_remote_copy(
            src_ref=src,
            dst_ref=dst,
            send_sem=csend.at[i],
            recv_sem=crecv.at[i],
            device_id=partner,
            device_id_type=MESH,
        )

    def halves(x):
        return [x[:, 0:LANES], x[:, LANES : 2 * LANES]]

    def strided(v, e):
        return pl.ds(2 * v + e, CHAN, stride=U)

    def put(t, v, values):
        for e, value in enumerate(halves(values)):
            stage[t, strided(v, e), :] = value

    def get(t, v):
        return jnp.concatenate([stage[t, strided(v, e), :] for e in range(2)], axis=1)

    def pack(t):
        tile_out[t] = stage[t].reshape(CHAN, U, LANES).astype(BF16)

    def unpack(t):
        stage[3 + t] = tile_in[t].astype(F32).reshape(CHAN * U, LANES)

    for load in loads[1:9]:
        load.wait()
    for t in range(2):
        for part in range(2):
            base = (2 * part + t) * CHAN
            piece = w_in_ref[:, base : base + CHAN]
            w_side[t, :, part * CHAN : part * CHAN + CHAN] = piece
            w_side_t[t, part * CHAN : part * CHAN + CHAN, :] = piece.astype(F32).T.astype(BF16)
    w_out_t[...] = w_out_ref[...].astype(F32).T.astype(BF16)
    w_gout_t[...] = w_gout_ref[...].astype(F32).T.astype(BF16)

    def column(ref):
        return jnp.broadcast_to(ref[...].reshape(1, CHAN), (8, CHAN)).T[:, 0:1]

    gain_in = column(gain_in_ref)
    bias_in = column(bias_in_ref)
    gain_out = column(gain_out_ref)
    bias_out = column(bias_out_ref)

    valid = jnp.broadcast_to(mask_ref[...].reshape(1, 512), (8, 512)).astype(F32).astype(BF16)
    number = lax.broadcasted_iota(jnp.int32, (512, WIDE), 0)
    place = lax.broadcasted_iota(jnp.int32, (512, WIDE), 1)
    col_pick = (number == col * TILE + place % 32).astype(F32).astype(BF16)
    col_valid = dot(valid, col_pick)
    for v in range(V):
        first = row * TILE + ((place // 32) % G) * U + place // LANES + 2 * v
        row_pick = (number == first).astype(F32).astype(BF16)
        masks[v] = (dot(valid, row_pick) * col_valid)[0:1, :]

    def branch(t, v, normed):
        mixed = dot(w_side_t[t], normed)
        projected = mixed[0:CHAN, :]
        gates = jax.nn.sigmoid(mixed[CHAN : 2 * CHAN, :])
        mask = masks[v]
        value = gates * projected * mask
        factor_s[t, v, 0:CHAN, :] = gates * mask
        factor_s[t, v, CHAN : 2 * CHAN, :] = value * (1.0 - gates)
        put(t, v, value)

    loads[0].wait()

    @pl.loop(0, V)
    def _(v):
        normed, scaled, inverse = normalize(tile_of(pair_ref, v), gain_in, bias_in)
        normed = normed.astype(BF16)
        normed_s[v] = normed
        scaled_s[v] = scaled
        inv_s[v] = inverse
        branch(1, v, normed)

    pack(1)
    pl.semaphore_wait(barrier, 15 + 15)

    @pl.loop(1, 16)
    def _(d):
        pl.semaphore_signal(ready_sem, inc=1, device_id=plane_peer(d), device_id_type=MESH)

    @pl.loop(0, V)
    def _(v):
        branch(0, v, normed_s[v])

    pack(0)
    pl.semaphore_wait(ready_sem, 15)
    send_owners(1)
    send_owners(0)

    loads[9].wait()

    @pl.loop(0, V)
    def _(v):
        ogate_s[v] = jax.nn.sigmoid(dot(w_gout_t[...], normed_s[v]))
        cot_s[v] = tile_of(cot_ref, v)

    owner_receive(1)
    for at, value in gather(1):
        right_m[core, :, at * LANES : at * LANES + LANES] = value
    right_copy = to_partner(0, right_m.at[core], right_m.at[core])
    right_copy.start()
    owner_receive(0)
    for at, value in gather(0):
        left_m[:, at * LANES : at * LANES + LANES] = value
    right_copy.wait_recv()
    for half in range(2):
        scatter(0, half, dot_nt(left_m[...], right_m[half]))
        send_tiles(0, half)
    tile_receive(0)

    unpack(0)

    @pl.loop(0, V)
    def _(v):
        out_norm, scaled, inverse = normalize(get(3, v), gain_out, bias_out)
        outer_proj = dot(w_out_t[...], out_norm.astype(BF16))
        gated = cot_s[v] * ogate_s[v]
        grad_outnorm = dot(w_out_ref[...], gated.astype(BF16))
        oproj_s[v] = outer_proj
        put(2, v, norm_back(grad_outnorm, gain_out, scaled, inverse))

    pack(2)
    send_owners(2)

    @pl.loop(0, V)
    def _(v):
        outer_proj = oproj_s[v]
        outer_gate = ogate_s[v]
        store_tile(out_ref, v, outer_gate * outer_proj)
        grad_gate = (cot_s[v] * outer_proj * outer_gate * (1.0 - outer_gate)).astype(BF16)
        ggate_s[v] = dot(w_gout_ref[...], grad_gate)

    owner_receive(2)
    for at, value in gather(2):
        grad_m[at // 2, :, (at % 2) * LANES : (at % 2) * LANES + LANES] = value

    def part(half):
        return slice(half * WIDE, half * WIDE + WIDE)

    def left_part(half):
        grad = dot(grad_m[0], right_m[0, :, part(half)])
        scatter(1, half, grad + dot(grad_m[1], right_m[1, :, part(half)]))
        send_tiles(1, half)

    left_part(0)
    swap_s[...] = dot_tn(grad_m[1 - core], left_m[...]).astype(BF16)
    grad_copy = to_partner(1, swap_s, swap_r)
    grad_copy.start()
    left_part(1)
    grad_copy.wait_recv()
    for half in range(2):
        grad = dot_tn(grad_m[core], left_m[:, part(half)])
        scatter(2, half, grad + swap_r[:, part(half)].astype(F32))
        send_tiles(2, half)

    def mixed(t, v):
        grad = get(4 + t, v)
        return jnp.concatenate([grad, grad], axis=0) * factor_s[t, v]

    tile_receive(1)
    unpack(1)

    @pl.loop(0, V)
    def _(v):
        ggate_s[v] += dot(w_side[0], mixed(0, v).astype(BF16))

    tile_receive(2)
    unpack(2)

    @pl.loop(0, V)
    def _(v):
        grad_normed = ggate_s[v] + dot(w_side[1], mixed(1, v).astype(BF16))
        store_tile(grad_ref, v, norm_back(grad_normed, gain_in, scaled_s[v], inv_s[v]))

    all_sent()
    right_copy.wait_send()
    grad_copy.wait_send()


def per_device(
    pair, residue_mask, cotangent, w_in, w_out, w_gout, gain_in, bias_in, gain_out, bias_out
):
    hbm = pl.BlockSpec(memory_space=pl.ANY)
    vmem = pl.BlockSpec(memory_space=pltpu.VMEM)
    shape = jax.ShapeDtypeStruct(pair.shape, BF16)
    args = (
        pair, residue_mask, cotangent, w_in, w_out, w_gout, gain_in, bias_in, gain_out, bias_out
    )
    return pl.pallas_call(
        kernel,
        out_shape=(shape, shape),
        in_specs=[hbm] * 10,
        out_specs=(vmem, vmem),
        scratch_shapes=[pltpu.VMEM(a.shape, a.dtype) for a in args]
        + [
            pltpu.VMEM((2, CHAN, 2 * CHAN), BF16),
            pltpu.VMEM((2, 2 * CHAN, CHAN), BF16),
            pltpu.VMEM((CHAN, CHAN), BF16),
            pltpu.VMEM((CHAN, CHAN), BF16),
            pltpu.VMEM((V, 1, WIDE), F32),
            pltpu.VMEM((V, CHAN, WIDE), BF16),
            pltpu.VMEM((V, CHAN, WIDE), F32),
            pltpu.VMEM((V, 1, WIDE), F32),
            pltpu.VMEM((2, V, 2 * CHAN, WIDE), F32),
            pltpu.VMEM((V, CHAN, WIDE), F32),
            pltpu.VMEM((V, CHAN, WIDE), F32),
            pltpu.VMEM((V, CHAN, WIDE), F32),
            pltpu.VMEM((V, CHAN, WIDE), F32),
            pltpu.VMEM((6, CHAN * U, LANES), F32),
            pltpu.VMEM((3, CHAN, U, LANES), BF16),
            pltpu.VMEM((3, CHAN, U, LANES), BF16),
            pltpu.VMEM((3, 8, 16, U, LANES), BF16),
            pltpu.VMEM((3, 8, 16, U, LANES), BF16),
            pltpu.VMEM((WIDE, 2 * WIDE), BF16),
            pltpu.VMEM((2, WIDE, 2 * WIDE), BF16),
            pltpu.VMEM((2, WIDE, WIDE), BF16),
            pltpu.VMEM((WIDE, 2 * WIDE), BF16),
            pltpu.VMEM((WIDE, 2 * WIDE), BF16),
            pltpu.SemaphoreType.DMA((3,)),
            pltpu.SemaphoreType.DMA((3,)),
            pltpu.SemaphoreType.DMA((3,)),
            pltpu.SemaphoreType.DMA((3,)),
            pltpu.SemaphoreType.DMA((2,)),
            pltpu.SemaphoreType.DMA((2,)),
            pltpu.SemaphoreType.DMA((10,)),
            pltpu.SemaphoreType.REGULAR,
        ],
        compiler_params=pltpu.CompilerParams(
            collective_id=0, has_side_effects=True, vmem_limit_bytes=60 * 1024 * 1024
        ),
    )(*args)


def solution(mesh):
    tile = P("row", "col", None)
    return jax.shard_map(
        per_device,
        mesh=mesh,
        in_specs=(tile, P(), tile, P(), P(), P(), P(), P(), P(), P()),
        out_specs=(tile, tile),
        check_vma=False,
    )
```

```python
import jax
import jax.numpy as jnp
from jax import lax
from jax.experimental import pallas as pl
from jax.experimental.pallas import tpu as pltpu
from jax.sharding import PartitionSpec as P

epsilon = 1e-05
MESH = pl.DeviceIdType.MESH
F32 = jnp.float32
BF16 = jnp.bfloat16

U = 8
G = 4
V = 4
TILE = 32
LANES = 128
CHAN = 128
WIDE = 256


def dot(a, b):
    return lax.dot_general(a, b, (((1,), (0,)), ((), ())), preferred_element_type=F32)


def dot_nt(a, b):
    return lax.dot_general(a, b, (((1,), (1,)), ((), ())), preferred_element_type=F32)


def dot_tn(a, b):
    return lax.dot_general(a, b, (((0,), (0,)), ((), ())), preferred_element_type=F32)


def swap_groups(parts):
    lane = lax.broadcasted_iota(jnp.int32, parts[0].shape, 1)
    low = lane < 64
    even = (lane // 32) % 2 == 0
    half = [[None, None], [None, None]]
    for bit in range(2):
        a, b = parts[bit], parts[2 + bit]
        half[0][bit] = jnp.where(low, a, pltpu.roll(b, 64, 1))
        half[1][bit] = jnp.where(low, pltpu.roll(a, 64, 1), b)
    out = []
    for bit in range(2):
        a, b = half[bit]
        out.append(jnp.where(even, a, pltpu.roll(b, 32, 1)))
        out.append(jnp.where(even, pltpu.roll(a, 96, 1), b))
    return out


def normalize(values, gain, bias):
    average = jnp.mean(values, axis=0, keepdims=True)
    centred = values - average
    inverse = lax.rsqrt(jnp.mean(centred * centred, axis=0, keepdims=True) + epsilon)
    scaled = centred * inverse
    return scaled * gain + bias, scaled, inverse


def norm_back(grad, gain, scaled, inverse):
    s = grad * gain
    first = jnp.mean(s, axis=0, keepdims=True)
    second = jnp.mean(s * scaled, axis=0, keepdims=True)
    return (s - first - scaled * second) * inverse


def tile_of(ref, v):
    rows = [ref[g * U + 2 * v + e] for e in range(2) for g in range(G)]
    return jnp.concatenate(rows, axis=0).astype(F32).T


def store_tile(ref, v, values):
    whole = values.T.astype(BF16)
    for e in range(2):
        for g in range(G):
            at = (e * G + g) * TILE
            ref[g * U + 2 * v + e] = whole[at : at + TILE, :]


def kernel(
    pair_hbm, mask_hbm, cot_hbm, w_in_hbm, w_out_hbm, w_gout_hbm,
    gain_in_hbm, bias_in_hbm, gain_out_hbm, bias_out_hbm,
    out_ref, grad_ref,
    pair_ref, mask_ref, cot_ref, w_in_ref, w_out_ref, w_gout_ref,
    gain_in_ref, bias_in_ref, gain_out_ref, bias_out_ref,
    w_side, w_side_t, w_out_t, w_gout_t, masks, normed_s, scaled_s, inv_s,
    factor_s, ogate_s, cot_s, oproj_s, ggate_s,
    stage, tile_out, tile_in, owner_out, owner_in, left_m, right_m, grad_m, swap_s, swap_r,
    tile_send, tile_recv, owner_send, owner_recv, csend, crecv, local_sem, ready_sem,
):
    arrays = [
        (pair_hbm, pair_ref), (mask_hbm, mask_ref), (w_in_hbm, w_in_ref), (w_out_hbm, w_out_ref),
        (w_gout_hbm, w_gout_ref), (gain_in_hbm, gain_in_ref), (bias_in_hbm, bias_in_ref),
        (gain_out_hbm, gain_out_ref), (bias_out_hbm, bias_out_ref), (cot_hbm, cot_ref),
    ]
    loads = [
        pltpu.make_async_copy(src, dst, local_sem.at[i]) for i, (src, dst) in enumerate(arrays)
    ]
    for load in loads:
        load.start()

    row = lax.axis_index("row")
    col = lax.axis_index("col")
    z = row % 8
    x_hi = row // 8
    core = col % 2
    q = col // 2
    side = row % 2
    block = row // 2
    chan = row * 8 + q
    partner = (row, col + 1 - 2 * core)

    barrier = pltpu.get_barrier_semaphore()

    def plane_peer(d):
        peer = (x_hi * 8 + q + d) % 16
        return ((peer // 8) * 8 + z, (peer % 8) * 2 + core)

    @pl.loop(1, 16)
    def _(d):
        peer = (z * 2 + core + d) % 16
        where = (x_hi * 8 + peer // 2, q * 2 + peer % 2)
        pl.semaphore_signal(barrier, inc=1, device_id=where, device_id_type=MESH)

    @pl.loop(1, 16)
    def _(d):
        pl.semaphore_signal(barrier, inc=1, device_id=plane_peer(d), device_id_type=MESH)

    def to_owner(t, c):
        return pltpu.make_async_remote_copy(
            src_ref=tile_out.at[t, c],
            dst_ref=owner_in.at[t, block, col],
            send_sem=tile_send.at[t],
            recv_sem=owner_recv.at[t],
            device_id=(c // 8, (c % 8) * 2 + side),
            device_id_type=MESH,
        )

    def send_owners(t):
        @pl.when(side == core)
        def _():
            pltpu.make_async_copy(
                tile_out.at[t, chan], owner_in.at[t, block, col], owner_recv.at[t]
            ).start()

        @pl.when(side != core)
        def _():
            to_owner(t, chan).start()

        @pl.loop(1, 128)
        def _(d):
            to_owner(t, (chan + d) % 128).start()

    def to_tile(t, to_block, to_col):
        return pltpu.make_async_remote_copy(
            src_ref=owner_out.at[t, to_block, to_col],
            dst_ref=tile_in.at[t, chan],
            send_sem=owner_send.at[t],
            recv_sem=tile_recv.at[t],
            device_id=(to_block * 2 + core, to_col),
            device_id_type=MESH,
        )

    def send_tiles(t, half):
        own = jnp.logical_and(side == core, core == half)

        @pl.when(own)
        def _():
            pltpu.make_async_copy(
                owner_out.at[t, block, col], tile_in.at[t, chan], tile_recv.at[t]
            ).start()

        @pl.when(jnp.logical_not(own))
        def _():
            to_tile(t, block, q * 2 + half).start()

        @pl.loop(1, 64)
        def _(d):
            to = (block * 8 + q + d) % 64
            to_tile(t, to // 8, (to % 8) * 2 + half).start()

    def owner_receive(t):
        pltpu.make_async_copy(owner_out.at[t], owner_in.at[t], owner_recv.at[t]).wait()

    def tile_receive(t):
        pltpu.make_async_copy(tile_out.at[t], tile_in.at[t], tile_recv.at[t]).wait()

    def all_sent():
        for t in range(3):
            for ref, sem in ((tile_out.at[t], tile_send.at[t]), (owner_out.at[t], owner_send.at[t])):

                @pl.when(side != core)
                def _():
                    pltpu.make_async_copy(ref, ref, sem).wait()

            @pl.when(side == core)
            def _():
                ref = tile_out.at[t, pl.ds(0, 127)]
                pltpu.make_async_copy(ref, ref, tile_send.at[t]).wait()
                for part in (owner_out.at[t, pl.ds(0, 7)], owner_out.at[t, 7, pl.ds(0, 15)]):
                    pltpu.make_async_copy(part, part, owner_send.at[t]).wait()

    def gather(t):
        for at in range(4):
            parts = [
                owner_in[t, :, ((at % 2) * 4 + p) * 2 + at // 2].astype(F32).reshape(64, LANES)
                for p in range(4)
            ]
            moved = [m.reshape(8, 1, U, LANES) for m in swap_groups(parts)]
            yield at, jnp.concatenate(moved, axis=1).reshape(WIDE, LANES).astype(BF16)

    def scatter(t, half, values):
        for at in range(2):
            tiles = values[:, at * LANES : at * LANES + LANES].reshape(8, G, U, LANES)
            parts = [tiles[:, g].reshape(64, LANES) for g in range(G)]
            for p, moved in enumerate(swap_groups(parts)):
                owner_out[t, :, (at * 4 + p) * 2 + half] = moved.reshape(8, U, LANES).astype(BF16)

    def to_partner(i, src, dst):
        return pltpu.make_async_remote_copy(
            src_ref=src,
            dst_ref=dst,
            send_sem=csend.at[i],
            recv_sem=crecv.at[i],
            device_id=partner,
            device_id_type=MESH,
        )

    def halves(x):
        return [x[:, 0:LANES], x[:, LANES : 2 * LANES]]

    def strided(v, e):
        return pl.ds(2 * v + e, CHAN, stride=U)

    def put(t, v, values):
        for e, value in enumerate(halves(values)):
            stage[t, strided(v, e), :] = value

    def get(t, v):
        return jnp.concatenate([stage[t, strided(v, e), :] for e in range(2)], axis=1)

    def pack(t):
        tile_out[t] = stage[t].reshape(CHAN, U, LANES).astype(BF16)

    def unpack(t):
        stage[3 + t] = tile_in[t].astype(F32).reshape(CHAN * U, LANES)

    for load in loads[1:9]:
        load.wait()
    for t in range(2):
        for part in range(2):
            base = (2 * part + t) * CHAN
            piece = w_in_ref[:, base : base + CHAN]
            w_side[t, :, part * CHAN : part * CHAN + CHAN] = piece
            w_side_t[t, part * CHAN : part * CHAN + CHAN, :] = piece.astype(F32).T.astype(BF16)
    w_out_t[...] = w_out_ref[...].astype(F32).T.astype(BF16)
    w_gout_t[...] = w_gout_ref[...].astype(F32).T.astype(BF16)

    def column(ref):
        return jnp.broadcast_to(ref[...].reshape(1, CHAN), (8, CHAN)).T[:, 0:1]

    gain_in = column(gain_in_ref)
    bias_in = column(bias_in_ref)
    gain_out = column(gain_out_ref)
    bias_out = column(bias_out_ref)

    valid = jnp.broadcast_to(mask_ref[...].reshape(1, 512), (8, 512)).astype(F32).astype(BF16)
    number = lax.broadcasted_iota(jnp.int32, (512, WIDE), 0)
    place = lax.broadcasted_iota(jnp.int32, (512, WIDE), 1)
    col_pick = (number == col * TILE + place % 32).astype(F32).astype(BF16)
    col_valid = dot(valid, col_pick)
    for v in range(V):
        first = row * TILE + ((place // 32) % G) * U + place // LANES + 2 * v
        row_pick = (number == first).astype(F32).astype(BF16)
        masks[v] = (dot(valid, row_pick) * col_valid)[0:1, :]

    def branch(t, v, normed):
        mixed = dot(w_side_t[t], normed)
        projected = mixed[0:CHAN, :]
        gates = jax.nn.sigmoid(mixed[CHAN : 2 * CHAN, :])
        mask = masks[v]
        value = gates * projected * mask
        factor_s[t, v, 0:CHAN, :] = gates * mask
        factor_s[t, v, CHAN : 2 * CHAN, :] = value * (1.0 - gates)
        put(t, v, value)

    loads[0].wait()

    @pl.loop(0, V, unroll=True)
    def _(v):
        normed, scaled, inverse = normalize(tile_of(pair_ref, v), gain_in, bias_in)
        normed = normed.astype(BF16)
        normed_s[v] = normed
        scaled_s[v] = scaled
        inv_s[v] = inverse
        branch(1, v, normed)

    pack(1)
    pl.semaphore_wait(barrier, 15 + 15)

    @pl.loop(1, 16)
    def _(d):
        pl.semaphore_signal(ready_sem, inc=1, device_id=plane_peer(d), device_id_type=MESH)

    @pl.loop(0, V, unroll=True)
    def _(v):
        branch(0, v, normed_s[v])

    pack(0)
    pl.semaphore_wait(ready_sem, 15)
    send_owners(1)
    send_owners(0)

    loads[9].wait()

    @pl.loop(0, V, unroll=True)
    def _(v):
        ogate_s[v] = jax.nn.sigmoid(dot(w_gout_t[...], normed_s[v]))
        cot_s[v] = tile_of(cot_ref, v)

    owner_receive(1)
    for at, value in gather(1):
        right_m[core, :, at * LANES : at * LANES + LANES] = value
    right_copy = to_partner(0, right_m.at[core], right_m.at[core])
    right_copy.start()
    owner_receive(0)
    for at, value in gather(0):
        left_m[:, at * LANES : at * LANES + LANES] = value
    right_copy.wait_recv()
    for half in range(2):
        scatter(0, half, dot_nt(left_m[...], right_m[half]))
        send_tiles(0, half)
    tile_receive(0)

    unpack(0)

    @pl.loop(0, V, unroll=True)
    def _(v):
        out_norm, scaled, inverse = normalize(get(3, v), gain_out, bias_out)
        outer_proj = dot(w_out_t[...], out_norm.astype(BF16))
        gated = cot_s[v] * ogate_s[v]
        grad_outnorm = dot(w_out_ref[...], gated.astype(BF16))
        oproj_s[v] = outer_proj
        put(2, v, norm_back(grad_outnorm, gain_out, scaled, inverse))

    pack(2)
    send_owners(2)

    @pl.loop(0, V, unroll=True)
    def _(v):
        outer_proj = oproj_s[v]
        outer_gate = ogate_s[v]
        store_tile(out_ref, v, outer_gate * outer_proj)
        grad_gate = (cot_s[v] * outer_proj * outer_gate * (1.0 - outer_gate)).astype(BF16)
        ggate_s[v] = dot(w_gout_ref[...], grad_gate)

    owner_receive(2)
    for at, value in gather(2):
        grad_m[at // 2, :, (at % 2) * LANES : (at % 2) * LANES + LANES] = value

    def part(half):
        return slice(half * WIDE, half * WIDE + WIDE)

    def left_part(half):
        grad = dot(grad_m[0], right_m[0, :, part(half)])
        scatter(1, half, grad + dot(grad_m[1], right_m[1, :, part(half)]))
        send_tiles(1, half)

    left_part(0)
    swap_s[...] = dot_tn(grad_m[1 - core], left_m[...]).astype(BF16)
    grad_copy = to_partner(1, swap_s, swap_r)
    grad_copy.start()
    left_part(1)
    grad_copy.wait_recv()
    for half in range(2):
        grad = dot_tn(grad_m[core], left_m[:, part(half)])
        scatter(2, half, grad + swap_r[:, part(half)].astype(F32))
        send_tiles(2, half)

    def mixed(t, v):
        grad = get(4 + t, v)
        return jnp.concatenate([grad, grad], axis=0) * factor_s[t, v]

    tile_receive(1)
    unpack(1)

    @pl.loop(0, V, unroll=True)
    def _(v):
        ggate_s[v] += dot(w_side[0], mixed(0, v).astype(BF16))

    tile_receive(2)
    unpack(2)

    @pl.loop(0, V, unroll=True)
    def _(v):
        grad_normed = ggate_s[v] + dot(w_side[1], mixed(1, v).astype(BF16))
        store_tile(grad_ref, v, norm_back(grad_normed, gain_in, scaled_s[v], inv_s[v]))

    all_sent()
    right_copy.wait_send()
    grad_copy.wait_send()


def per_device(
    pair, residue_mask, cotangent, w_in, w_out, w_gout, gain_in, bias_in, gain_out, bias_out
):
    hbm = pl.BlockSpec(memory_space=pl.ANY)
    vmem = pl.BlockSpec(memory_space=pltpu.VMEM)
    shape = jax.ShapeDtypeStruct(pair.shape, BF16)
    args = (
        pair, residue_mask, cotangent, w_in, w_out, w_gout, gain_in, bias_in, gain_out, bias_out
    )
    return pl.pallas_call(
        kernel,
        out_shape=(shape, shape),
        in_specs=[hbm] * 10,
        out_specs=(vmem, vmem),
        scratch_shapes=[pltpu.VMEM(a.shape, a.dtype) for a in args]
        + [
            pltpu.VMEM((2, CHAN, 2 * CHAN), BF16),
            pltpu.VMEM((2, 2 * CHAN, CHAN), BF16),
            pltpu.VMEM((CHAN, CHAN), BF16),
            pltpu.VMEM((CHAN, CHAN), BF16),
            pltpu.VMEM((V, 1, WIDE), F32),
            pltpu.VMEM((V, CHAN, WIDE), BF16),
            pltpu.VMEM((V, CHAN, WIDE), F32),
            pltpu.VMEM((V, 1, WIDE), F32),
            pltpu.VMEM((2, V, 2 * CHAN, WIDE), F32),
            pltpu.VMEM((V, CHAN, WIDE), F32),
            pltpu.VMEM((V, CHAN, WIDE), F32),
            pltpu.VMEM((V, CHAN, WIDE), F32),
            pltpu.VMEM((V, CHAN, WIDE), F32),
            pltpu.VMEM((6, CHAN * U, LANES), F32),
            pltpu.VMEM((3, CHAN, U, LANES), BF16),
            pltpu.VMEM((3, CHAN, U, LANES), BF16),
            pltpu.VMEM((3, 8, 16, U, LANES), BF16),
            pltpu.VMEM((3, 8, 16, U, LANES), BF16),
            pltpu.VMEM((WIDE, 2 * WIDE), BF16),
            pltpu.VMEM((2, WIDE, 2 * WIDE), BF16),
            pltpu.VMEM((2, WIDE, WIDE), BF16),
            pltpu.VMEM((WIDE, 2 * WIDE), BF16),
            pltpu.VMEM((WIDE, 2 * WIDE), BF16),
            pltpu.SemaphoreType.DMA((3,)),
            pltpu.SemaphoreType.DMA((3,)),
            pltpu.SemaphoreType.DMA((3,)),
            pltpu.SemaphoreType.DMA((3,)),
            pltpu.SemaphoreType.DMA((2,)),
            pltpu.SemaphoreType.DMA((2,)),
            pltpu.SemaphoreType.DMA((10,)),
            pltpu.SemaphoreType.REGULAR,
        ],
        compiler_params=pltpu.CompilerParams(
            collective_id=0, has_side_effects=True, vmem_limit_bytes=48 * 1024 * 1024
        ),
    )(*[pltpu.with_memory_space_constraint(a, pltpu.HBM) for a in args])


def solution(mesh):
    tile = P("row", "col", None)
    return jax.shard_map(
        per_device,
        mesh=mesh,
        in_specs=(tile, P(), tile, P(), P(), P(), P(), P(), P(), P()),
        out_specs=(tile, tile),
        check_vma=False,
    )
```

```python
import jax
import jax.numpy as jnp
from jax import lax
from jax.experimental import pallas as pl
from jax.experimental.pallas import tpu as pltpu
from jax.sharding import PartitionSpec as P

epsilon = 1e-05
MESH = pl.DeviceIdType.MESH
F32 = jnp.float32
BF16 = jnp.bfloat16

U = 8
G = 4
V = 4
TILE = 32
LANES = 128
CHAN = 128
WIDE = 256


def dot(a, b):
    return lax.dot_general(a, b, (((1,), (0,)), ((), ())), preferred_element_type=F32)


def dot_nt(a, b):
    return lax.dot_general(a, b, (((1,), (1,)), ((), ())), preferred_element_type=F32)


def dot_tn(a, b):
    return lax.dot_general(a, b, (((0,), (0,)), ((), ())), preferred_element_type=F32)


def swap_groups(parts):
    lane = lax.broadcasted_iota(jnp.int32, parts[0].shape, 1)
    low = lane < 64
    even = (lane // 32) % 2 == 0
    half = [[None, None], [None, None]]
    for bit in range(2):
        a, b = parts[bit], parts[2 + bit]
        half[0][bit] = jnp.where(low, a, pltpu.roll(b, 64, 1))
        half[1][bit] = jnp.where(low, pltpu.roll(a, 64, 1), b)
    out = []
    for bit in range(2):
        a, b = half[bit]
        out.append(jnp.where(even, a, pltpu.roll(b, 32, 1)))
        out.append(jnp.where(even, pltpu.roll(a, 96, 1), b))
    return out


def normalize(values, gain, bias):
    average = jnp.mean(values, axis=0, keepdims=True)
    centred = values - average
    inverse = lax.rsqrt(jnp.mean(centred * centred, axis=0, keepdims=True) + epsilon)
    scaled = centred * inverse
    return scaled * gain + bias, scaled, inverse


def norm_back(grad, gain, scaled, inverse):
    s = grad * gain
    first = jnp.mean(s, axis=0, keepdims=True)
    second = jnp.mean(s * scaled, axis=0, keepdims=True)
    return (s - first - scaled * second) * inverse


def tile_of(ref, v):
    rows = [ref[g * U + 2 * v + e] for e in range(2) for g in range(G)]
    return jnp.concatenate(rows, axis=0).astype(F32).T


def store_tile(ref, v, values):
    whole = values.T.astype(BF16)
    for e in range(2):
        for g in range(G):
            at = (e * G + g) * TILE
            ref[g * U + 2 * v + e] = whole[at : at + TILE, :]


def kernel(
    pair_hbm, mask_hbm, cot_hbm, w_in_hbm, w_out_hbm, w_gout_hbm,
    gain_in_hbm, bias_in_hbm, gain_out_hbm, bias_out_hbm,
    out_ref, grad_ref,
    pair_ref, mask_ref, cot_ref, w_in_ref, w_out_ref, w_gout_ref,
    gain_in_ref, bias_in_ref, gain_out_ref, bias_out_ref,
    w_side, w_side_t, w_out_t, w_gout_t, masks, normed_s, scaled_s, inv_s,
    factor_s, ogate_s, cot_s, oproj_s, ggate_s,
    stage, tile_out, tile_in, owner_out, owner_in, left_m, right_m, grad_m, swap_s, swap_r, left_s,
    tile_send, tile_recv, owner_send, owner_recv, csend, crecv, local_sem, ready_sem,
):
    arrays = [
        (pair_hbm, pair_ref), (mask_hbm, mask_ref), (w_in_hbm, w_in_ref), (w_out_hbm, w_out_ref),
        (w_gout_hbm, w_gout_ref), (gain_in_hbm, gain_in_ref), (bias_in_hbm, bias_in_ref),
        (gain_out_hbm, gain_out_ref), (bias_out_hbm, bias_out_ref), (cot_hbm, cot_ref),
    ]
    loads = [
        pltpu.make_async_copy(src, dst, local_sem.at[i]) for i, (src, dst) in enumerate(arrays)
    ]
    for load in loads:
        load.start()

    row = lax.axis_index("row")
    col = lax.axis_index("col")
    z = row % 8
    x_hi = row // 8
    core = col % 2
    q = col // 2
    side = row % 2
    block = row // 2
    chan = row * 8 + q
    partner = (row, col + 1 - 2 * core)

    barrier = pltpu.get_barrier_semaphore()

    def plane_peer(d):
        peer = (x_hi * 8 + q + d) % 16
        return ((peer // 8) * 8 + z, (peer % 8) * 2 + core)

    @pl.loop(1, 16)
    def _(d):
        peer = (z * 2 + core + d) % 16
        where = (x_hi * 8 + peer // 2, q * 2 + peer % 2)
        pl.semaphore_signal(barrier, inc=1, device_id=where, device_id_type=MESH)

    @pl.loop(1, 16)
    def _(d):
        pl.semaphore_signal(barrier, inc=1, device_id=plane_peer(d), device_id_type=MESH)

    def to_owner(t, c):
        return pltpu.make_async_remote_copy(
            src_ref=tile_out.at[t, c],
            dst_ref=owner_in.at[t, block, col],
            send_sem=tile_send.at[t],
            recv_sem=owner_recv.at[t, col // 8],
            device_id=(c // 8, (c % 8) * 2 + side),
            device_id_type=MESH,
        )

    def send_owners(t):
        @pl.when(side == core)
        def _():
            pltpu.make_async_copy(
                tile_out.at[t, chan], owner_in.at[t, block, col], owner_recv.at[t, col // 8]
            ).start()

        @pl.when(side != core)
        def _():
            to_owner(t, chan).start()

        @pl.loop(1, 128)
        def _(d):
            to_owner(t, (chan + d) % 128).start()

    def to_tile(t, to_block, to_col):
        return pltpu.make_async_remote_copy(
            src_ref=owner_out.at[t, to_block, to_col],
            dst_ref=tile_in.at[t, chan],
            send_sem=owner_send.at[t],
            recv_sem=tile_recv.at[t],
            device_id=(to_block * 2 + core, to_col),
            device_id_type=MESH,
        )

    def send_some(t, own, to_block, to_col, where, count):
        @pl.when(own)
        def _():
            pltpu.make_async_copy(
                owner_out.at[t, block, col], tile_in.at[t, chan], tile_recv.at[t]
            ).start()

        @pl.when(jnp.logical_not(own))
        def _():
            to_tile(t, to_block, to_col).start()

        @pl.loop(1, count)
        def _(d):
            to_tile(t, *where(d)).start()

    def send_part(t, at):
        p, h = at // 2, at % 2

        def where(d):
            to = (block * 4 + q % 4 + d) % 32
            return to // 4, (h * 4 + to % 4) * 2 + p

        own = jnp.logical_and(side == core, jnp.logical_and(q // 4 == h, core == p))
        send_some(t, own, block, (h * 4 + q % 4) * 2 + p, where, 32)

    def send_blocks(t, half):
        def where(d):
            to = ((block % 4) * 16 + col + d) % 64
            return half * 4 + to // 16, to % 16

        own = jnp.logical_and(side == core, block // 4 == half)
        send_some(t, own, half * 4 + block % 4, col, where, 64)

    def owner_receive(t, parts=(0, 1)):
        for h in parts:
            ref = owner_in.at[t, :, pl.ds(h * 8, 8)]
            pltpu.make_async_copy(ref, ref, owner_recv.at[t, h]).wait()

    def tile_receive(t):
        pltpu.make_async_copy(tile_out.at[t], tile_in.at[t], tile_recv.at[t]).wait()

    def all_sent():
        for t in range(3):
            for ref, sem in ((tile_out.at[t], tile_send.at[t]), (owner_out.at[t], owner_send.at[t])):

                @pl.when(side != core)
                def _():
                    pltpu.make_async_copy(ref, ref, sem).wait()

            @pl.when(side == core)
            def _():
                ref = tile_out.at[t, pl.ds(0, 127)]
                pltpu.make_async_copy(ref, ref, tile_send.at[t]).wait()
                for part in (owner_out.at[t, pl.ds(0, 7)], owner_out.at[t, 7, pl.ds(0, 15)]):
                    pltpu.make_async_copy(part, part, owner_send.at[t]).wait()

    def gather(t, at):
        parts = [
            owner_in[t, :, ((at % 2) * 4 + p) * 2 + at // 2].astype(F32).reshape(64, LANES)
            for p in range(4)
        ]
        moved = [m.reshape(8, 1, U, LANES) for m in swap_groups(parts)]
        return jnp.concatenate(moved, axis=1).reshape(WIDE, LANES).astype(BF16)

    def scatter(t, at, values, blocks=slice(0, 8)):
        count = values.shape[0] // TILE
        tiles = values.reshape(count, G, U, LANES)
        parts = [tiles[:, g].reshape(count * U, LANES) for g in range(G)]
        for p, moved in enumerate(swap_groups(parts)):
            to = ((at % 2) * 4 + p) * 2 + at // 2
            owner_out[t, blocks, to] = moved.reshape(count, U, LANES).astype(BF16)

    def lanes(at):
        return slice(at * LANES, at * LANES + LANES)

    def to_partner(i, src, dst):
        return pltpu.make_async_remote_copy(
            src_ref=src,
            dst_ref=dst,
            send_sem=csend.at[i],
            recv_sem=crecv.at[i],
            device_id=partner,
            device_id_type=MESH,
        )

    def halves(x):
        return [x[:, 0:LANES], x[:, LANES : 2 * LANES]]

    def strided(v, e):
        return pl.ds(2 * v + e, CHAN, stride=U)

    def put(t, v, values):
        for e, value in enumerate(halves(values)):
            stage[t, strided(v, e), :] = value

    def get(t, v):
        return jnp.concatenate([stage[t, strided(v, e), :] for e in range(2)], axis=1)

    def pack(t):
        tile_out[t] = stage[t].reshape(CHAN, U, LANES).astype(BF16)

    def unpack(t):
        stage[3 + t] = tile_in[t].astype(F32).reshape(CHAN * U, LANES)

    for load in loads[1:9]:
        load.wait()
    for t in range(2):
        for part in range(2):
            base = (2 * part + t) * CHAN
            piece = w_in_ref[:, base : base + CHAN]
            w_side[t, :, part * CHAN : part * CHAN + CHAN] = piece
            w_side_t[t, part * CHAN : part * CHAN + CHAN, :] = piece.astype(F32).T.astype(BF16)
    w_out_t[...] = w_out_ref[...].astype(F32).T.astype(BF16)
    w_gout_t[...] = w_gout_ref[...].astype(F32).T.astype(BF16)

    def column(ref):
        return jnp.broadcast_to(ref[...].reshape(1, CHAN), (8, CHAN)).T[:, 0:1]

    gain_in = column(gain_in_ref)
    bias_in = column(bias_in_ref)
    gain_out = column(gain_out_ref)
    bias_out = column(bias_out_ref)

    valid = jnp.broadcast_to(mask_ref[...].reshape(1, 512), (8, 512)).astype(F32).astype(BF16)
    number = lax.broadcasted_iota(jnp.int32, (512, WIDE), 0)
    place = lax.broadcasted_iota(jnp.int32, (512, WIDE), 1)
    col_pick = (number == col * TILE + place % 32).astype(F32).astype(BF16)
    col_valid = dot(valid, col_pick)
    for v in range(V):
        first = row * TILE + ((place // 32) % G) * U + place // LANES + 2 * v
        row_pick = (number == first).astype(F32).astype(BF16)
        masks[v] = (dot(valid, row_pick) * col_valid)[0:1, :]

    def branch(t, v, normed):
        mixed = dot(w_side_t[t], normed)
        projected = mixed[0:CHAN, :]
        gates = jax.nn.sigmoid(mixed[CHAN : 2 * CHAN, :])
        mask = masks[v]
        value = gates * projected * mask
        factor_s[t, v, 0:CHAN, :] = gates * mask
        factor_s[t, v, CHAN : 2 * CHAN, :] = value * (1.0 - gates)
        put(t, v, value)

    loads[0].wait()

    @pl.loop(0, V, unroll=True)
    def _(v):
        normed, scaled, inverse = normalize(tile_of(pair_ref, v), gain_in, bias_in)
        normed = normed.astype(BF16)
        normed_s[v] = normed
        scaled_s[v] = scaled
        inv_s[v] = inverse
        branch(1, v, normed)

    pack(1)
    pl.semaphore_wait(barrier, 15 + 15)

    @pl.loop(1, 16)
    def _(d):
        pl.semaphore_signal(ready_sem, inc=1, device_id=plane_peer(d), device_id_type=MESH)

    @pl.loop(0, V, unroll=True)
    def _(v):
        branch(0, v, normed_s[v])

    pack(0)
    pl.semaphore_wait(ready_sem, 15)
    send_owners(1)
    send_owners(0)

    loads[9].wait()

    @pl.loop(0, V, unroll=True)
    def _(v):
        ogate_s[v] = jax.nn.sigmoid(dot(w_gout_t[...], normed_s[v]))
        cot_s[v] = tile_of(cot_ref, v)

    owner_receive(1)
    for at in range(4):
        value = gather(1, at)
        for h in range(2):
            right_m[core, h, :, lanes(at)] = value[h * LANES : h * LANES + LANES, :]
    right_copy = to_partner(0, right_m.at[core], right_m.at[core])
    right_copy.start()
    owner_receive(0)
    for at in range(4):
        left_m[:, lanes(at)] = gather(0, at)
    right_copy.wait_recv()

    def right_rows(h):
        return jnp.concatenate([right_m[0, h], right_m[1, h]], axis=0)

    for h in range(2):
        for p in range(2):
            scatter(0, 2 * p + h, dot_nt(left_m[...], right_m[p, h]))
            send_part(0, 2 * p + h)
    tile_receive(0)

    unpack(0)

    @pl.loop(0, V, unroll=True)
    def _(v):
        out_norm, scaled, inverse = normalize(get(3, v), gain_out, bias_out)
        outer_proj = dot(w_out_t[...], out_norm.astype(BF16))
        gated = cot_s[v] * ogate_s[v]
        grad_outnorm = dot(w_out_ref[...], gated.astype(BF16))
        oproj_s[v] = outer_proj
        put(2, v, norm_back(grad_outnorm, gain_out, scaled, inverse))

    pack(2)
    send_owners(2)

    @pl.loop(0, V, unroll=True)
    def _(v):
        outer_proj = oproj_s[v]
        outer_gate = ogate_s[v]
        store_tile(out_ref, v, outer_gate * outer_proj)
        grad_gate = (cot_s[v] * outer_proj * outer_gate * (1.0 - outer_gate)).astype(BF16)
        ggate_s[v] = dot(w_gout_ref[...], grad_gate)

    def grad_rows(h):
        return jnp.concatenate([grad_m[h, 0], grad_m[h, 1]], axis=1)

    grad_copies = [to_partner(1 + h, swap_s.at[h], swap_r.at[h]) for h in range(2)]

    def swap_right(h):
        swap_s[h] = dot_tn(grad_m[h, 1 - core], left_m[...]).astype(BF16)
        grad_copies[h].start()

    def send_right(h):
        grad = dot_tn(grad_m[h, core], left_m[...])
        grad_copies[h].wait_recv()
        grad = grad + swap_r[h].astype(F32)
        for at in range(4):
            scatter(2, at, grad[:, lanes(at)], slice(4 * h, 4 * h + 4))
        send_blocks(2, h)

    owner_receive(2, (0,))
    for p in range(2):
        grad_m[0, p] = gather(2, 2 * p)
    swap_right(0)
    left_s[...] = dot(grad_rows(0), right_rows(0))
    send_right(0)
    owner_receive(2, (1,))
    for p in range(2):
        grad_m[1, p] = gather(2, 2 * p + 1)
    for at in range(4):
        grad = dot(grad_rows(1), right_rows(1)[:, lanes(at)])
        scatter(1, at, left_s[:, lanes(at)] + grad)
        send_part(1, at)
        if at == 0:
            swap_right(1)
    send_right(1)

    def mixed(t, v):
        grad = get(4 + t, v)
        return jnp.concatenate([grad, grad], axis=0) * factor_s[t, v]

    tile_receive(1)
    unpack(1)

    @pl.loop(0, V, unroll=True)
    def _(v):
        ggate_s[v] += dot(w_side[0], mixed(0, v).astype(BF16))

    tile_receive(2)
    unpack(2)

    @pl.loop(0, V, unroll=True)
    def _(v):
        grad_normed = ggate_s[v] + dot(w_side[1], mixed(1, v).astype(BF16))
        store_tile(grad_ref, v, norm_back(grad_normed, gain_in, scaled_s[v], inv_s[v]))

    all_sent()
    for copy in [right_copy] + grad_copies:
        copy.wait_send()


def per_device(
    pair, residue_mask, cotangent, w_in, w_out, w_gout, gain_in, bias_in, gain_out, bias_out
):
    hbm = pl.BlockSpec(memory_space=pl.ANY)
    vmem = pl.BlockSpec(memory_space=pltpu.VMEM)
    shape = jax.ShapeDtypeStruct(pair.shape, BF16)
    args = (
        pair, residue_mask, cotangent, w_in, w_out, w_gout, gain_in, bias_in, gain_out, bias_out
    )
    return pl.pallas_call(
        kernel,
        out_shape=(shape, shape),
        in_specs=[hbm] * 10,
        out_specs=(vmem, vmem),
        scratch_shapes=[pltpu.VMEM(a.shape, a.dtype) for a in args]
        + [
            pltpu.VMEM((2, CHAN, 2 * CHAN), BF16),
            pltpu.VMEM((2, 2 * CHAN, CHAN), BF16),
            pltpu.VMEM((CHAN, CHAN), BF16),
            pltpu.VMEM((CHAN, CHAN), BF16),
            pltpu.VMEM((V, 1, WIDE), F32),
            pltpu.VMEM((V, CHAN, WIDE), BF16),
            pltpu.VMEM((V, CHAN, WIDE), F32),
            pltpu.VMEM((V, 1, WIDE), F32),
            pltpu.VMEM((2, V, 2 * CHAN, WIDE), F32),
            pltpu.VMEM((V, CHAN, WIDE), F32),
            pltpu.VMEM((V, CHAN, WIDE), F32),
            pltpu.VMEM((V, CHAN, WIDE), F32),
            pltpu.VMEM((V, CHAN, WIDE), F32),
            pltpu.VMEM((6, CHAN * U, LANES), F32),
            pltpu.VMEM((3, CHAN, U, LANES), BF16),
            pltpu.VMEM((3, CHAN, U, LANES), BF16),
            pltpu.VMEM((3, 8, 16, U, LANES), BF16),
            pltpu.VMEM((3, 8, 16, U, LANES), BF16),
            pltpu.VMEM((WIDE, 2 * WIDE), BF16),
            pltpu.VMEM((2, 2, LANES, 2 * WIDE), BF16),
            pltpu.VMEM((2, 2, WIDE, LANES), BF16),
            pltpu.VMEM((2, LANES, 2 * WIDE), BF16),
            pltpu.VMEM((2, LANES, 2 * WIDE), BF16),
            pltpu.VMEM((WIDE, 2 * WIDE), F32),
            pltpu.SemaphoreType.DMA((3,)),
            pltpu.SemaphoreType.DMA((3,)),
            pltpu.SemaphoreType.DMA((3,)),
            pltpu.SemaphoreType.DMA((3, 2)),
            pltpu.SemaphoreType.DMA((3,)),
            pltpu.SemaphoreType.DMA((3,)),
            pltpu.SemaphoreType.DMA((10,)),
            pltpu.SemaphoreType.REGULAR,
        ],
        compiler_params=pltpu.CompilerParams(
            collective_id=0, has_side_effects=True, vmem_limit_bytes=48 * 1024 * 1024
        ),
    )(*[pltpu.with_memory_space_constraint(a, pltpu.HBM) for a in args])


def solution(mesh):
    tile = P("row", "col", None)
    return jax.shard_map(
        per_device,
        mesh=mesh,
        in_specs=(tile, P(), tile, P(), P(), P(), P(), P(), P(), P()),
        out_specs=(tile, tile),
        check_vma=False,
    )
```

```python
import jax
import jax.numpy as jnp
from jax import lax
from jax.experimental import pallas as pl
from jax.experimental.pallas import tpu as pltpu
from jax.sharding import PartitionSpec as P

epsilon = 1e-05
MESH = pl.DeviceIdType.MESH
F32 = jnp.float32
BF16 = jnp.bfloat16

U = 8
G = 4
V = 4
TILE = 32
LANES = 128
CHAN = 128
WIDE = 256


def dot(a, b):
    return lax.dot_general(a, b, (((1,), (0,)), ((), ())), preferred_element_type=F32)


def dot_nt(a, b):
    return lax.dot_general(a, b, (((1,), (1,)), ((), ())), preferred_element_type=F32)


def dot_tn(a, b):
    return lax.dot_general(a, b, (((0,), (0,)), ((), ())), preferred_element_type=F32)


def swap_groups(parts):
    lane = lax.broadcasted_iota(jnp.int32, parts[0].shape, 1)
    low = lane < 64
    even = (lane // 32) % 2 == 0
    half = [[None, None], [None, None]]
    for bit in range(2):
        a, b = parts[bit], parts[2 + bit]
        half[0][bit] = jnp.where(low, a, pltpu.roll(b, 64, 1))
        half[1][bit] = jnp.where(low, pltpu.roll(a, 64, 1), b)
    out = []
    for bit in range(2):
        a, b = half[bit]
        out.append(jnp.where(even, a, pltpu.roll(b, 32, 1)))
        out.append(jnp.where(even, pltpu.roll(a, 96, 1), b))
    return out


def normalize(values, gain, bias):
    average = jnp.mean(values, axis=0, keepdims=True)
    centred = values - average
    inverse = lax.rsqrt(jnp.mean(centred * centred, axis=0, keepdims=True) + epsilon)
    scaled = centred * inverse
    return scaled * gain + bias, scaled, inverse


def norm_back(grad, gain, scaled, inverse):
    s = grad * gain
    first = jnp.mean(s, axis=0, keepdims=True)
    second = jnp.mean(s * scaled, axis=0, keepdims=True)
    return (s - first - scaled * second) * inverse


def tile_of(ref, v):
    rows = [ref[g * U + 2 * v + e] for e in range(2) for g in range(G)]
    return jnp.concatenate(rows, axis=0).astype(F32).T


def store_tile(ref, v, values):
    whole = values.T.astype(BF16)
    for e in range(2):
        for g in range(G):
            at = (e * G + g) * TILE
            ref[g * U + 2 * v + e] = whole[at : at + TILE, :]


def kernel(
    pair_hbm, mask_hbm, cot_hbm, w_in_hbm, w_out_hbm, w_gout_hbm,
    gain_in_hbm, bias_in_hbm, gain_out_hbm, bias_out_hbm,
    out_ref, grad_ref,
    pair_ref, mask_ref, cot_ref, w_in_ref, w_out_ref, w_gout_ref,
    gain_in_ref, bias_in_ref, gain_out_ref, bias_out_ref,
    w_side, w_side_t, w_out_t, w_gout_t, masks, normed_s, scaled_s, inv_s,
    factor_s, ogate_s, cot_s, oproj_s, ggate_s,
    stage, tile_out, tile_in, owner_out, owner_in, left_m, right_m, grad_m, swap_s, swap_r, left_s,
    tile_send, tile_recv, owner_send, owner_recv, csend, crecv, local_sem, ready_sem,
):
    arrays = [
        (pair_hbm, pair_ref), (mask_hbm, mask_ref), (w_in_hbm, w_in_ref), (w_out_hbm, w_out_ref),
        (w_gout_hbm, w_gout_ref), (gain_in_hbm, gain_in_ref), (bias_in_hbm, bias_in_ref),
        (gain_out_hbm, gain_out_ref), (bias_out_hbm, bias_out_ref), (cot_hbm, cot_ref),
    ]
    loads = [
        pltpu.make_async_copy(src, dst, local_sem.at[i]) for i, (src, dst) in enumerate(arrays)
    ]
    for load in loads:
        load.start()

    row = lax.axis_index("row")
    col = lax.axis_index("col")
    z = row % 8
    x_hi = row // 8
    core = col % 2
    q = col // 2
    side = row % 2
    block = row // 2
    chan = row * 8 + q
    partner = (row, col + 1 - 2 * core)

    barrier = pltpu.get_barrier_semaphore()

    def plane_peer(d):
        peer = (x_hi * 8 + q + d) % 16
        return ((peer // 8) * 8 + z, (peer % 8) * 2 + core)

    @pl.loop(1, 16)
    def _(d):
        peer = (z * 2 + core + d) % 16
        where = (x_hi * 8 + peer // 2, q * 2 + peer % 2)
        pl.semaphore_signal(barrier, inc=1, device_id=where, device_id_type=MESH)

    @pl.loop(1, 16)
    def _(d):
        pl.semaphore_signal(barrier, inc=1, device_id=plane_peer(d), device_id_type=MESH)

    def to_owner(t, c):
        return pltpu.make_async_remote_copy(
            src_ref=tile_out.at[t, c],
            dst_ref=owner_in.at[t, block, col],
            send_sem=tile_send.at[t],
            recv_sem=owner_recv.at[t, col // 8],
            device_id=(c // 8, (c % 8) * 2 + side),
            device_id_type=MESH,
        )

    def send_owners(t):
        @pl.when(side == core)
        def _():
            pltpu.make_async_copy(
                tile_out.at[t, chan], owner_in.at[t, block, col], owner_recv.at[t, col // 8]
            ).start()

        @pl.when(side != core)
        def _():
            to_owner(t, chan).start()

        @pl.loop(1, 128)
        def _(d):
            to_owner(t, (chan + d) % 128).start()

    def to_tile(t, to_block, to_col):
        return pltpu.make_async_remote_copy(
            src_ref=owner_out.at[t, to_block, to_col],
            dst_ref=tile_in.at[t, chan],
            send_sem=owner_send.at[t],
            recv_sem=tile_recv.at[t],
            device_id=(to_block * 2 + core, to_col),
            device_id_type=MESH,
        )

    def send_some(t, own, to_block, to_col, where, count):
        @pl.when(own)
        def _():
            pltpu.make_async_copy(
                owner_out.at[t, block, col], tile_in.at[t, chan], tile_recv.at[t]
            ).start()

        @pl.when(jnp.logical_not(own))
        def _():
            to_tile(t, to_block, to_col).start()

        @pl.loop(1, count)
        def _(d):
            to_tile(t, *where(d)).start()

    def send_part(t, at):
        p, h = at // 2, at % 2

        def where(d):
            to = (block * 4 + q % 4 + d) % 32
            return to // 4, (h * 4 + to % 4) * 2 + p

        own = jnp.logical_and(side == core, jnp.logical_and(q // 4 == h, core == p))
        send_some(t, own, block, (h * 4 + q % 4) * 2 + p, where, 32)

    def send_blocks(t, half):
        def where(d):
            to = ((block % 4) * 16 + col + d) % 64
            return half * 4 + to // 16, to % 16

        own = jnp.logical_and(side == core, block // 4 == half)
        send_some(t, own, half * 4 + block % 4, col, where, 64)

    def owner_receive(t, parts=(0, 1)):
        for h in parts:
            ref = owner_in.at[t, :, pl.ds(h * 8, 8)]
            pltpu.make_async_copy(ref, ref, owner_recv.at[t, h]).wait()

    def tile_receive(t):
        pltpu.make_async_copy(tile_out.at[t], tile_in.at[t], tile_recv.at[t]).wait()

    def all_sent():
        for t in range(3):
            for ref, sem in ((tile_out.at[t], tile_send.at[t]), (owner_out.at[t], owner_send.at[t])):

                @pl.when(side != core)
                def _():
                    pltpu.make_async_copy(ref, ref, sem).wait()

            @pl.when(side == core)
            def _():
                ref = tile_out.at[t, pl.ds(0, 127)]
                pltpu.make_async_copy(ref, ref, tile_send.at[t]).wait()
                for part in (owner_out.at[t, pl.ds(0, 7)], owner_out.at[t, 7, pl.ds(0, 15)]):
                    pltpu.make_async_copy(part, part, owner_send.at[t]).wait()

    def gather(t, at):
        parts = [
            owner_in[t, :, ((at % 2) * 4 + p) * 2 + at // 2].astype(F32).reshape(64, LANES)
            for p in range(4)
        ]
        moved = [m.reshape(8, 1, U, LANES) for m in swap_groups(parts)]
        return jnp.concatenate(moved, axis=1).reshape(WIDE, LANES).astype(BF16)

    def scatter(t, at, values, blocks=slice(0, 8)):
        count = values.shape[0] // TILE
        tiles = values.reshape(count, G, U, LANES)
        parts = [tiles[:, g].reshape(count * U, LANES) for g in range(G)]
        for p, moved in enumerate(swap_groups(parts)):
            to = ((at % 2) * 4 + p) * 2 + at // 2
            owner_out[t, blocks, to] = moved.reshape(count, U, LANES).astype(BF16)

    def lanes(at):
        return slice(at * LANES, at * LANES + LANES)

    def to_partner(i, src, dst):
        return pltpu.make_async_remote_copy(
            src_ref=src,
            dst_ref=dst,
            send_sem=csend.at[i],
            recv_sem=crecv.at[i],
            device_id=partner,
            device_id_type=MESH,
        )

    def halves(x):
        return [x[:, 0:LANES], x[:, LANES : 2 * LANES]]

    def strided(v, e):
        return pl.ds(2 * v + e, CHAN, stride=U)

    def put(t, v, values):
        for e, value in enumerate(halves(values)):
            stage[t, strided(v, e), :] = value

    def get(t, v):
        return jnp.concatenate([stage[t, strided(v, e), :] for e in range(2)], axis=1)

    def pack(t):
        tile_out[t] = stage[t, 0 : CHAN * U].reshape(CHAN, U, LANES).astype(BF16)

    def unpack(t):
        stage[3 + t, 0 : CHAN * U] = tile_in[t].astype(F32).reshape(CHAN * U, LANES)

    for load in loads[1:9]:
        load.wait()
    for t in range(2):
        for part in range(2):
            base = (2 * part + t) * CHAN
            piece = w_in_ref[:, base : base + CHAN]
            w_side[t, :, part * CHAN : part * CHAN + CHAN] = piece
            w_side_t[t, part * CHAN : part * CHAN + CHAN, :] = piece.astype(F32).T.astype(BF16)
    w_out_t[...] = w_out_ref[...].astype(F32).T.astype(BF16)
    w_gout_t[...] = w_gout_ref[...].astype(F32).T.astype(BF16)

    def column(ref):
        return jnp.broadcast_to(ref[...].reshape(1, CHAN), (8, CHAN)).T[:, 0:1]

    gain_in = column(gain_in_ref)
    bias_in = column(bias_in_ref)
    gain_out = column(gain_out_ref)
    bias_out = column(bias_out_ref)

    valid = jnp.broadcast_to(mask_ref[...].reshape(1, 512), (8, 512)).astype(F32).astype(BF16)
    number = lax.broadcasted_iota(jnp.int32, (512, WIDE), 0)
    place = lax.broadcasted_iota(jnp.int32, (512, WIDE), 1)
    col_pick = (number == col * TILE + place % 32).astype(F32).astype(BF16)
    col_valid = dot(valid, col_pick)
    for v in range(V):
        first = row * TILE + ((place // 32) % G) * U + place // LANES + 2 * v
        row_pick = (number == first).astype(F32).astype(BF16)
        masks[v] = (dot(valid, row_pick) * col_valid)[0:1, :]

    def branch(t, v, normed):
        mixed = dot(w_side_t[t], normed)
        projected = mixed[0:CHAN, :]
        gates = jax.nn.sigmoid(mixed[CHAN : 2 * CHAN, :])
        mask = masks[v]
        value = gates * projected * mask
        factor_s[t, v, 0:CHAN, :] = gates * mask
        factor_s[t, v, CHAN : 2 * CHAN, :] = value * (1.0 - gates)
        put(t, v, value)

    loads[0].wait()

    @pl.loop(0, V, unroll=True)
    def _(v):
        normed, scaled, inverse = normalize(tile_of(pair_ref, v), gain_in, bias_in)
        normed = normed.astype(BF16)
        normed_s[v] = normed
        scaled_s[v] = scaled
        inv_s[v] = inverse
        branch(1, v, normed)

    pack(1)
    pl.semaphore_wait(barrier, 15 + 15)

    @pl.loop(1, 16)
    def _(d):
        pl.semaphore_signal(ready_sem, inc=1, device_id=plane_peer(d), device_id_type=MESH)

    @pl.loop(0, V, unroll=True)
    def _(v):
        branch(0, v, normed_s[v])

    pack(0)
    pl.semaphore_wait(ready_sem, 15)
    send_owners(1)
    send_owners(0)

    loads[9].wait()

    @pl.loop(0, V, unroll=True)
    def _(v):
        ogate_s[v] = jax.nn.sigmoid(dot(w_gout_t[...], normed_s[v]))
        cot_s[v] = tile_of(cot_ref, v)

    owner_receive(1)
    for at in range(4):
        value = gather(1, at)
        for h in range(2):
            right_m[core, h, :, lanes(at)] = value[h * LANES : h * LANES + LANES, :]
    right_copy = to_partner(0, right_m.at[core], right_m.at[core])
    right_copy.start()
    owner_receive(0)
    for at in range(4):
        left_m[:, lanes(at)] = gather(0, at)
    right_copy.wait_recv()

    def right_rows(h):
        return jnp.concatenate([right_m[0, h], right_m[1, h]], axis=0)

    for h in range(2):
        for p in range(2):
            scatter(0, 2 * p + h, dot_nt(left_m[...], right_m[p, h]))
            send_part(0, 2 * p + h)
    tile_receive(0)

    unpack(0)

    @pl.loop(0, V, unroll=True)
    def _(v):
        out_norm, scaled, inverse = normalize(get(3, v), gain_out, bias_out)
        outer_proj = dot(w_out_t[...], out_norm.astype(BF16))
        gated = cot_s[v] * ogate_s[v]
        grad_outnorm = dot(w_out_ref[...], gated.astype(BF16))
        oproj_s[v] = outer_proj
        put(2, v, norm_back(grad_outnorm, gain_out, scaled, inverse))

    pack(2)
    send_owners(2)

    @pl.loop(0, V, unroll=True)
    def _(v):
        outer_proj = oproj_s[v]
        outer_gate = ogate_s[v]
        store_tile(out_ref, v, outer_gate * outer_proj)
        grad_gate = (cot_s[v] * outer_proj * outer_gate * (1.0 - outer_gate)).astype(BF16)
        ggate_s[v] = dot(w_gout_ref[...], grad_gate)

    def grad_rows(h):
        return jnp.concatenate([grad_m[h, 0], grad_m[h, 1]], axis=1)

    grad_copies = [to_partner(1 + h, swap_s.at[h], swap_r.at[h]) for h in range(2)]

    def swap_right(h):
        swap_s[h] = dot_tn(grad_m[h, 1 - core], left_m[...]).astype(BF16)
        grad_copies[h].start()

    def send_right(h):
        grad = dot_tn(grad_m[h, core], left_m[...])
        grad_copies[h].wait_recv()
        grad = grad + swap_r[h].astype(F32)
        for at in range(4):
            scatter(2, at, grad[:, lanes(at)], slice(4 * h, 4 * h + 4))
        send_blocks(2, h)

    owner_receive(2, (0,))
    for p in range(2):
        grad_m[0, p] = gather(2, 2 * p)
    swap_right(0)
    left_s[...] = dot(grad_rows(0), right_rows(0))
    send_right(0)
    owner_receive(2, (1,))
    for p in range(2):
        grad_m[1, p] = gather(2, 2 * p + 1)
    for at in range(4):
        grad = dot(grad_rows(1), right_rows(1)[:, lanes(at)])
        scatter(1, at, left_s[:, lanes(at)] + grad)
        send_part(1, at)
        if at == 0:
            swap_right(1)
    send_right(1)

    def mixed(t, v):
        grad = get(4 + t, v)
        return jnp.concatenate([grad, grad], axis=0) * factor_s[t, v]

    tile_receive(1)
    unpack(1)

    @pl.loop(0, V, unroll=True)
    def _(v):
        ggate_s[v] += dot(w_side[0], mixed(0, v).astype(BF16))

    tile_receive(2)
    unpack(2)

    @pl.loop(0, V, unroll=True)
    def _(v):
        grad_normed = ggate_s[v] + dot(w_side[1], mixed(1, v).astype(BF16))
        store_tile(grad_ref, v, norm_back(grad_normed, gain_in, scaled_s[v], inv_s[v]))

    all_sent()
    for copy in [right_copy] + grad_copies:
        copy.wait_send()


def per_device(
    pair, residue_mask, cotangent, w_in, w_out, w_gout, gain_in, bias_in, gain_out, bias_out
):
    hbm = pl.BlockSpec(memory_space=pl.ANY)
    vmem = pl.BlockSpec(memory_space=pltpu.VMEM)
    shape = jax.ShapeDtypeStruct(pair.shape, BF16)
    args = (
        pair, residue_mask, cotangent, w_in, w_out, w_gout, gain_in, bias_in, gain_out, bias_out
    )
    return pl.pallas_call(
        kernel,
        out_shape=(shape, shape),
        in_specs=[hbm] * 10,
        out_specs=(vmem, vmem),
        scratch_shapes=[pltpu.VMEM(a.shape, a.dtype) for a in args]
        + [
            pltpu.VMEM((2, CHAN, 2 * CHAN), BF16),
            pltpu.VMEM((2, 2 * CHAN, CHAN), BF16),
            pltpu.VMEM((CHAN, CHAN), BF16),
            pltpu.VMEM((CHAN, CHAN), BF16),
            pltpu.VMEM((V, 1, WIDE), F32),
            pltpu.VMEM((V, CHAN, WIDE), BF16),
            pltpu.VMEM((V, CHAN, WIDE), F32),
            pltpu.VMEM((V, 1, WIDE), F32),
            pltpu.VMEM((2, V, 2 * CHAN, WIDE), F32),
            pltpu.VMEM((V, CHAN, WIDE), F32),
            pltpu.VMEM((V, CHAN, WIDE), F32),
            pltpu.VMEM((V, CHAN, WIDE), F32),
            pltpu.VMEM((V, CHAN, WIDE), F32),
            pltpu.VMEM((6, CHAN * U + U, LANES), F32),
            pltpu.VMEM((3, CHAN, U, LANES), BF16),
            pltpu.VMEM((3, CHAN, U, LANES), BF16),
            pltpu.VMEM((3, 8, 16, U, LANES), BF16),
            pltpu.VMEM((3, 8, 16, U, LANES), BF16),
            pltpu.VMEM((WIDE, 2 * WIDE), BF16),
            pltpu.VMEM((2, 2, LANES, 2 * WIDE), BF16),
            pltpu.VMEM((2, 2, WIDE, LANES), BF16),
            pltpu.VMEM((2, LANES, 2 * WIDE), BF16),
            pltpu.VMEM((2, LANES, 2 * WIDE), BF16),
            pltpu.VMEM((WIDE, 2 * WIDE), F32),
            pltpu.SemaphoreType.DMA((3,)),
            pltpu.SemaphoreType.DMA((3,)),
            pltpu.SemaphoreType.DMA((3,)),
            pltpu.SemaphoreType.DMA((3, 2)),
            pltpu.SemaphoreType.DMA((3,)),
            pltpu.SemaphoreType.DMA((3,)),
            pltpu.SemaphoreType.DMA((10,)),
            pltpu.SemaphoreType.REGULAR,
        ],
        compiler_params=pltpu.CompilerParams(
            collective_id=0, has_side_effects=True, vmem_limit_bytes=48 * 1024 * 1024
        ),
    )(*[pltpu.with_memory_space_constraint(a, pltpu.HBM) for a in args])


def solution(mesh):
    tile = P("row", "col", None)
    return jax.shard_map(
        per_device,
        mesh=mesh,
        in_specs=(tile, P(), tile, P(), P(), P(), P(), P(), P(), P()),
        out_specs=(tile, tile),
        check_vma=False,
    )
```

```python
import jax
import jax.numpy as jnp
from jax import lax
from jax.experimental import pallas as pl
from jax.experimental.pallas import tpu as pltpu
from jax.sharding import PartitionSpec as P

epsilon = 1e-05
MESH = pl.DeviceIdType.MESH
F32 = jnp.float32
BF16 = jnp.bfloat16

U = 8
G = 4
V = 4
TILE = 32
LANES = 128
CHAN = 128
WIDE = 256


def dot(a, b):
    return lax.dot_general(a, b, (((1,), (0,)), ((), ())), preferred_element_type=F32)


def dot_nt(a, b):
    return lax.dot_general(a, b, (((1,), (1,)), ((), ())), preferred_element_type=F32)


def dot_tn(a, b):
    return lax.dot_general(a, b, (((0,), (0,)), ((), ())), preferred_element_type=F32)


def swap_groups(parts):
    lane = lax.broadcasted_iota(jnp.int32, parts[0].shape, 1)
    low = lane < 64
    even = (lane // 32) % 2 == 0
    half = [[None, None], [None, None]]
    for bit in range(2):
        a, b = parts[bit], parts[2 + bit]
        half[0][bit] = jnp.where(low, a, pltpu.roll(b, 64, 1))
        half[1][bit] = jnp.where(low, pltpu.roll(a, 64, 1), b)
    out = []
    for bit in range(2):
        a, b = half[bit]
        out.append(jnp.where(even, a, pltpu.roll(b, 32, 1)))
        out.append(jnp.where(even, pltpu.roll(a, 96, 1), b))
    return out


def normalize(values, gain, bias):
    average = jnp.mean(values, axis=0, keepdims=True)
    centred = values - average
    inverse = lax.rsqrt(jnp.mean(centred * centred, axis=0, keepdims=True) + epsilon)
    scaled = centred * inverse
    return scaled * gain + bias, scaled, inverse


def norm_back(grad, gain, scaled, inverse):
    s = grad * gain
    first = jnp.mean(s, axis=0, keepdims=True)
    second = jnp.mean(s * scaled, axis=0, keepdims=True)
    return (s - first - scaled * second) * inverse


def tile_of(ref, v):
    rows = [ref[g * U + 2 * v + e] for e in range(2) for g in range(G)]
    return jnp.concatenate(rows, axis=0).astype(F32).T


def store_tile(ref, v, values):
    whole = values.T.astype(BF16)
    for e in range(2):
        for g in range(G):
            at = (e * G + g) * TILE
            ref[g * U + 2 * v + e] = whole[at : at + TILE, :]


def kernel(
    pair_hbm, mask_hbm, cot_hbm, w_in_hbm, w_out_hbm, w_gout_hbm,
    gain_in_hbm, bias_in_hbm, gain_out_hbm, bias_out_hbm,
    out_ref, grad_ref,
    pair_ref, mask_ref, cot_ref, w_in_ref, w_out_ref, w_gout_ref,
    gain_in_ref, bias_in_ref, gain_out_ref, bias_out_ref,
    w_side, w_side_t, w_out_t, w_gout_t, masks, normed_s, scaled_s, inv_s,
    factor_s, ogate_s, cot_s, oproj_s, ggate_s,
    stage, tile_out, tile_in, owner_out, owner_in, left_m, right_m, grad_m, swap_s, swap_r, left_s,
    tile_send, tile_recv, owner_send, owner_recv, csend, crecv, local_sem, ready_sem,
):
    arrays = [
        (pair_hbm, pair_ref), (mask_hbm, mask_ref), (w_in_hbm, w_in_ref), (w_out_hbm, w_out_ref),
        (w_gout_hbm, w_gout_ref), (gain_in_hbm, gain_in_ref), (bias_in_hbm, bias_in_ref),
        (gain_out_hbm, gain_out_ref), (bias_out_hbm, bias_out_ref), (cot_hbm, cot_ref),
    ]
    loads = [
        pltpu.make_async_copy(src, dst, local_sem.at[i]) for i, (src, dst) in enumerate(arrays)
    ]
    for load in loads:
        load.start()

    row = lax.axis_index("row")
    col = lax.axis_index("col")
    z = row % 8
    x_hi = row // 8
    core = col % 2
    q = col // 2
    side = row % 2
    block = row // 2
    chan = row * 8 + q
    partner = (row, col + 1 - 2 * core)

    barrier = pltpu.get_barrier_semaphore()

    def plane_peer(d):
        peer = (x_hi * 8 + q + d) % 16
        return ((peer // 8) * 8 + z, (peer % 8) * 2 + core)

    @pl.loop(1, 16)
    def _(d):
        peer = (z * 2 + core + d) % 16
        where = (x_hi * 8 + peer // 2, q * 2 + peer % 2)
        pl.semaphore_signal(barrier, inc=1, device_id=where, device_id_type=MESH)

    @pl.loop(1, 16)
    def _(d):
        pl.semaphore_signal(barrier, inc=1, device_id=plane_peer(d), device_id_type=MESH)

    def to_owner(t, c):
        return pltpu.make_async_remote_copy(
            src_ref=tile_out.at[t, c],
            dst_ref=owner_in.at[t, block, col],
            send_sem=tile_send.at[t],
            recv_sem=owner_recv.at[t, col // 8],
            device_id=(c // 8, (c % 8) * 2 + side),
            device_id_type=MESH,
        )

    def send_owners(t):
        @pl.when(side == core)
        def _():
            pltpu.make_async_copy(
                tile_out.at[t, chan], owner_in.at[t, block, col], owner_recv.at[t, col // 8]
            ).start()

        @pl.when(side != core)
        def _():
            to_owner(t, chan).start()

        @pl.loop(1, 128)
        def _(d):
            to_owner(t, (chan + d) % 128).start()

    def to_tile(t, to_block, to_col):
        return pltpu.make_async_remote_copy(
            src_ref=owner_out.at[t, to_block, to_col],
            dst_ref=tile_in.at[t, chan],
            send_sem=owner_send.at[t],
            recv_sem=tile_recv.at[t],
            device_id=(to_block * 2 + core, to_col),
            device_id_type=MESH,
        )

    def send_some(t, own, to_block, to_col, where, count):
        @pl.when(own)
        def _():
            pltpu.make_async_copy(
                owner_out.at[t, block, col], tile_in.at[t, chan], tile_recv.at[t]
            ).start()

        @pl.when(jnp.logical_not(own))
        def _():
            to_tile(t, to_block, to_col).start()

        @pl.loop(1, count)
        def _(d):
            to_tile(t, *where(d)).start()

    def send_part(t, at):
        p, h = at // 2, at % 2

        def where(d):
            to = (block * 4 + q % 4 + d) % 32
            return to // 4, (h * 4 + to % 4) * 2 + p

        own = jnp.logical_and(side == core, jnp.logical_and(q // 4 == h, core == p))
        send_some(t, own, block, (h * 4 + q % 4) * 2 + p, where, 32)

    def send_blocks(t, half, at):
        p, h = at // 2, at % 2

        def where(d):
            to = ((block % 4) * 4 + q % 4 + d) % 16
            return half * 4 + to // 4, (h * 4 + to % 4) * 2 + p

        own = jnp.logical_and(block // 4 == half, jnp.logical_and(q // 4 == h, core == p))
        own = jnp.logical_and(side == core, own)
        send_some(t, own, half * 4 + block % 4, (h * 4 + q % 4) * 2 + p, where, 16)

    def owner_receive(t, parts=(0, 1)):
        for h in parts:
            ref = owner_in.at[t, :, pl.ds(h * 8, 8)]
            pltpu.make_async_copy(ref, ref, owner_recv.at[t, h]).wait()

    def tile_receive(t):
        pltpu.make_async_copy(tile_out.at[t], tile_in.at[t], tile_recv.at[t]).wait()

    def all_sent():
        for t in range(3):
            for ref, sem in ((tile_out.at[t], tile_send.at[t]), (owner_out.at[t], owner_send.at[t])):

                @pl.when(side != core)
                def _():
                    pltpu.make_async_copy(ref, ref, sem).wait()

            @pl.when(side == core)
            def _():
                ref = tile_out.at[t, pl.ds(0, 127)]
                pltpu.make_async_copy(ref, ref, tile_send.at[t]).wait()
                for part in (owner_out.at[t, pl.ds(0, 7)], owner_out.at[t, 7, pl.ds(0, 15)]):
                    pltpu.make_async_copy(part, part, owner_send.at[t]).wait()

    def gather(t, at):
        parts = [
            owner_in[t, :, ((at % 2) * 4 + p) * 2 + at // 2].astype(F32).reshape(64, LANES)
            for p in range(4)
        ]
        moved = [m.reshape(8, 1, U, LANES) for m in swap_groups(parts)]
        return jnp.concatenate(moved, axis=1).reshape(WIDE, LANES).astype(BF16)

    def scatter(t, at, values, blocks=slice(0, 8)):
        count = values.shape[0] // TILE
        tiles = values.reshape(count, G, U, LANES)
        parts = [tiles[:, g].reshape(count * U, LANES) for g in range(G)]
        for p, moved in enumerate(swap_groups(parts)):
            to = ((at % 2) * 4 + p) * 2 + at // 2
            owner_out[t, blocks, to] = moved.reshape(count, U, LANES).astype(BF16)

    def lanes(at):
        return slice(at * LANES, at * LANES + LANES)

    def to_partner(i, src, dst):
        return pltpu.make_async_remote_copy(
            src_ref=src,
            dst_ref=dst,
            send_sem=csend.at[i],
            recv_sem=crecv.at[i],
            device_id=partner,
            device_id_type=MESH,
        )

    def halves(x):
        return [x[:, 0:LANES], x[:, LANES : 2 * LANES]]

    def strided(v, e):
        return pl.ds(2 * v + e, CHAN, stride=U)

    def put(t, v, values):
        for e, value in enumerate(halves(values)):
            stage[t, strided(v, e), :] = value

    def get(t, v):
        return jnp.concatenate([stage[t, strided(v, e), :] for e in range(2)], axis=1)

    def pack(t):
        tile_out[t] = stage[t, 0 : CHAN * U].reshape(CHAN, U, LANES).astype(BF16)

    def unpack(t):
        stage[3 + t, 0 : CHAN * U] = tile_in[t].astype(F32).reshape(CHAN * U, LANES)

    for load in loads[1:9]:
        load.wait()
    for t in range(2):
        for part in range(2):
            base = (2 * part + t) * CHAN
            piece = w_in_ref[:, base : base + CHAN]
            w_side[t, :, part * CHAN : part * CHAN + CHAN] = piece
            w_side_t[t, part * CHAN : part * CHAN + CHAN, :] = piece.astype(F32).T.astype(BF16)
    w_out_t[...] = w_out_ref[...].astype(F32).T.astype(BF16)
    w_gout_t[...] = w_gout_ref[...].astype(F32).T.astype(BF16)

    def column(ref):
        return jnp.broadcast_to(ref[...].reshape(1, CHAN), (8, CHAN)).T[:, 0:1]

    gain_in = column(gain_in_ref)
    bias_in = column(bias_in_ref)
    gain_out = column(gain_out_ref)
    bias_out = column(bias_out_ref)

    valid = jnp.broadcast_to(mask_ref[...].reshape(1, 512), (8, 512)).astype(F32).astype(BF16)
    number = lax.broadcasted_iota(jnp.int32, (512, WIDE), 0)
    place = lax.broadcasted_iota(jnp.int32, (512, WIDE), 1)
    col_pick = (number == col * TILE + place % 32).astype(F32).astype(BF16)
    col_valid = dot(valid, col_pick)
    for v in range(V):
        first = row * TILE + ((place // 32) % G) * U + place // LANES + 2 * v
        row_pick = (number == first).astype(F32).astype(BF16)
        masks[v] = (dot(valid, row_pick) * col_valid)[0:1, :]

    def branch(t, v, normed):
        mixed = dot(w_side_t[t], normed)
        projected = mixed[0:CHAN, :]
        gates = jax.nn.sigmoid(mixed[CHAN : 2 * CHAN, :])
        mask = masks[v]
        value = gates * projected * mask
        factor_s[t, v, 0:CHAN, :] = gates * mask
        factor_s[t, v, CHAN : 2 * CHAN, :] = value * (1.0 - gates)
        put(t, v, value)

    loads[0].wait()

    @pl.loop(0, V, unroll=True)
    def _(v):
        normed, scaled, inverse = normalize(tile_of(pair_ref, v), gain_in, bias_in)
        normed = normed.astype(BF16)
        normed_s[v] = normed
        scaled_s[v] = scaled
        inv_s[v] = inverse
        branch(1, v, normed)

    pack(1)
    pl.semaphore_wait(barrier, 15 + 15)

    @pl.loop(1, 16)
    def _(d):
        pl.semaphore_signal(ready_sem, inc=1, device_id=plane_peer(d), device_id_type=MESH)

    @pl.loop(0, V, unroll=True)
    def _(v):
        branch(0, v, normed_s[v])

    pack(0)
    pl.semaphore_wait(ready_sem, 15)
    send_owners(1)
    send_owners(0)

    loads[9].wait()

    @pl.loop(0, V, unroll=True)
    def _(v):
        ogate_s[v] = jax.nn.sigmoid(dot(w_gout_t[...], normed_s[v]))
        cot_s[v] = tile_of(cot_ref, v)

    owner_receive(1)
    for at in range(4):
        value = gather(1, at)
        for h in range(2):
            right_m[core, h, :, lanes(at)] = value[h * LANES : h * LANES + LANES, :]
    right_copy = to_partner(0, right_m.at[core], right_m.at[core])
    right_copy.start()
    owner_receive(0)
    for at in range(4):
        left_m[:, lanes(at)] = gather(0, at)
    right_copy.wait_recv()

    def right_rows(h):
        return jnp.concatenate([right_m[0, h], right_m[1, h]], axis=0)

    for h in range(2):
        for p in range(2):
            scatter(0, 2 * p + h, dot_nt(left_m[...], right_m[p, h]))
            send_part(0, 2 * p + h)
    tile_receive(0)

    unpack(0)

    @pl.loop(0, V, unroll=True)
    def _(v):
        out_norm, scaled, inverse = normalize(get(3, v), gain_out, bias_out)
        outer_proj = dot(w_out_t[...], out_norm.astype(BF16))
        gated = cot_s[v] * ogate_s[v]
        grad_outnorm = dot(w_out_ref[...], gated.astype(BF16))
        oproj_s[v] = outer_proj
        put(2, v, norm_back(grad_outnorm, gain_out, scaled, inverse))

    pack(2)
    send_owners(2)

    @pl.loop(0, V, unroll=True)
    def _(v):
        outer_proj = oproj_s[v]
        outer_gate = ogate_s[v]
        store_tile(out_ref, v, outer_gate * outer_proj)
        grad_gate = (cot_s[v] * outer_proj * outer_gate * (1.0 - outer_gate)).astype(BF16)
        ggate_s[v] = dot(w_gout_ref[...], grad_gate)

    def grad_rows(h):
        return jnp.concatenate([grad_m[h, 0], grad_m[h, 1]], axis=1)

    grad_copies = [to_partner(1 + h, swap_s.at[h], swap_r.at[h]) for h in range(2)]

    def swap_right(h):
        swap_s[h] = dot_tn(grad_m[h, 1 - core], left_m[...]).astype(BF16)
        grad_copies[h].start()

    def send_right(h):
        for at in range(4):
            grad = dot_tn(grad_m[h, core], left_m[:, lanes(at)])
            if at == 0:
                grad_copies[h].wait_recv()
            grad = grad + swap_r[h, :, lanes(at)].astype(F32)
            scatter(2, at, grad, slice(4 * h, 4 * h + 4))
            send_blocks(2, h, at)

    owner_receive(2, (0,))
    for p in range(2):
        grad_m[0, p] = gather(2, 2 * p)
    swap_right(0)
    left_s[...] = dot(grad_rows(0), right_rows(0))
    send_right(0)
    owner_receive(2, (1,))
    for p in range(2):
        grad_m[1, p] = gather(2, 2 * p + 1)
    for at in range(4):
        grad = dot(grad_rows(1), right_rows(1)[:, lanes(at)])
        scatter(1, at, left_s[:, lanes(at)] + grad)
        send_part(1, at)
        if at == 0:
            swap_right(1)
    send_right(1)

    def mixed(t, v):
        grad = get(4 + t, v)
        return jnp.concatenate([grad, grad], axis=0) * factor_s[t, v]

    tile_receive(1)
    unpack(1)

    @pl.loop(0, V, unroll=True)
    def _(v):
        ggate_s[v] += dot(w_side[0], mixed(0, v).astype(BF16))

    tile_receive(2)
    unpack(2)

    @pl.loop(0, V, unroll=True)
    def _(v):
        grad_normed = ggate_s[v] + dot(w_side[1], mixed(1, v).astype(BF16))
        store_tile(grad_ref, v, norm_back(grad_normed, gain_in, scaled_s[v], inv_s[v]))

    all_sent()
    for copy in [right_copy] + grad_copies:
        copy.wait_send()


def per_device(
    pair, residue_mask, cotangent, w_in, w_out, w_gout, gain_in, bias_in, gain_out, bias_out
):
    hbm = pl.BlockSpec(memory_space=pl.ANY)
    vmem = pl.BlockSpec(memory_space=pltpu.VMEM)
    shape = jax.ShapeDtypeStruct(pair.shape, BF16)
    args = (
        pair, residue_mask, cotangent, w_in, w_out, w_gout, gain_in, bias_in, gain_out, bias_out
    )
    return pl.pallas_call(
        kernel,
        out_shape=(shape, shape),
        in_specs=[hbm] * 10,
        out_specs=(vmem, vmem),
        scratch_shapes=[pltpu.VMEM(a.shape, a.dtype) for a in args]
        + [
            pltpu.VMEM((2, CHAN, 2 * CHAN), BF16),
            pltpu.VMEM((2, 2 * CHAN, CHAN), BF16),
            pltpu.VMEM((CHAN, CHAN), BF16),
            pltpu.VMEM((CHAN, CHAN), BF16),
            pltpu.VMEM((V, 1, WIDE), F32),
            pltpu.VMEM((V, CHAN, WIDE), BF16),
            pltpu.VMEM((V, CHAN, WIDE), F32),
            pltpu.VMEM((V, 1, WIDE), F32),
            pltpu.VMEM((2, V, 2 * CHAN, WIDE), F32),
            pltpu.VMEM((V, CHAN, WIDE), F32),
            pltpu.VMEM((V, CHAN, WIDE), F32),
            pltpu.VMEM((V, CHAN, WIDE), F32),
            pltpu.VMEM((V, CHAN, WIDE), F32),
            pltpu.VMEM((6, CHAN * U + U, LANES), F32),
            pltpu.VMEM((3, CHAN, U, LANES), BF16),
            pltpu.VMEM((3, CHAN, U, LANES), BF16),
            pltpu.VMEM((3, 8, 16, U, LANES), BF16),
            pltpu.VMEM((3, 8, 16, U, LANES), BF16),
            pltpu.VMEM((WIDE, 2 * WIDE), BF16),
            pltpu.VMEM((2, 2, LANES, 2 * WIDE), BF16),
            pltpu.VMEM((2, 2, WIDE, LANES), BF16),
            pltpu.VMEM((2, LANES, 2 * WIDE), BF16),
            pltpu.VMEM((2, LANES, 2 * WIDE), BF16),
            pltpu.VMEM((WIDE, 2 * WIDE), F32),
            pltpu.SemaphoreType.DMA((3,)),
            pltpu.SemaphoreType.DMA((3,)),
            pltpu.SemaphoreType.DMA((3,)),
            pltpu.SemaphoreType.DMA((3, 2)),
            pltpu.SemaphoreType.DMA((3,)),
            pltpu.SemaphoreType.DMA((3,)),
            pltpu.SemaphoreType.DMA((10,)),
            pltpu.SemaphoreType.REGULAR,
        ],
        compiler_params=pltpu.CompilerParams(
            collective_id=0, has_side_effects=True, vmem_limit_bytes=48 * 1024 * 1024
        ),
    )(*[pltpu.with_memory_space_constraint(a, pltpu.HBM) for a in args])


def solution(mesh):
    tile = P("row", "col", None)
    return jax.shard_map(
        per_device,
        mesh=mesh,
        in_specs=(tile, P(), tile, P(), P(), P(), P(), P(), P(), P()),
        out_specs=(tile, tile),
        check_vma=False,
    )
```
